32 devices in a mesh: phase: 4 (over y, core), axial: 2 (over x), radial: 4 (over z).
Axes of the slice: x: 2, y: 2, z: 4, core: 2. Of those that a mesh axis runs over, the one named last changes fastest.
Arguments:
- psi_start: float32 [4, 10, 8, 64, 128], P('phase', None, 'axial', 'radial'), may hold values from -6 to 6
- source: float32 [4, 10, 8, 64, 128], P('phase', None, 'axial', 'radial'), may hold values from -6 to 6
- face_coef: bfloat16 [6, 8, 64, 128], P(None, 'axial', 'radial'), may hold values from 0.099609375 to 1
- diag_coef: float32 [8, 64, 128], P('axial', 'radial'), may hold values from 6 to 10
- flux_jac: float32 [6, 2, 5, 5], replicated, may hold values from -2 to 2
- omega: float32 [1], replicated, may hold values from 0.5 to 2
- metric: float32 [3, 10], replicated, may hold values from -2 to 2
- mode_shape: bfloat16 [12, 3, 8, 64, 128], P(None, None, 'axial', 'radial'), may hold values from -6 to 6
- phase_weight: float32 [4], P('phase'), may hold values from 0.05 to 0.5
- pairing: int32 [2, 4, 64], P('axial', 'radial'), may hold values from 0 to 63, each once within a row
- owner_order: int32 [2, 4, 8192], P('axial', 'radial'), may hold values from 0 to 8191, each once within a row
Outputs:
- psi_out: float32 [4, 10, 8, 64, 128], P('phase', None, 'axial', 'radial')
- sens: float32 [12, 2, 4, 8192], P(None, 'axial', 'radial', 'phase')
The draws below stay inside these ranges and needn't reach their ends.
Inputs may be any that keep to these rules, and one draw needn't show every extreme that they name: `pairing`: each tile's row is a permutation of its pitch-end nodes. `owner_order`: each tile's row is a permutation of its cells.
All inputs are finite; a program needn't handle non-finite values.
Results may differ from the reference program's by a relative error of at most 0.0003.
Values sent between devices are 32-bit elements; how exact they have to be, the bound alone decides.
A program may use at most 64 MiB of HBM per device.

```python
import math
import jax
import jax.numpy as jnp
from jax import lax

FIELDS = 5
MODES = 12
BLADES = 16
ITERS = 4
NT = 128
PHASES = 4
NA = 8
NR = 64
FACE = 64
CELLS = 8192
N_AXIAL = 2
N_RADIAL = 4


def block_scale(key, dims, cuts, least, top_value):
    gain, own = 1.0, jax.random.fold_in(key, 6)
    for axis_at, blocks in cuts:
        draws = jnp.exp(jax.random.uniform(jax.random.fold_in(own, axis_at), (blocks,), jnp.float32, least / len(cuts), top_value / len(cuts)))
        gain = gain * jnp.repeat(draws, dims[axis_at] // blocks).reshape([-1 if axis == axis_at else 1 for axis in range(len(dims))])
    return gain


def bell_draw(rng, shape, spread, bound, shards=(), held_as=jnp.bfloat16):
    gain = block_scale(rng, shape, shards, -0.22, 0.18) if shards else 1.0
    result = jax.random.normal(rng, shape, jnp.float32) * spread * gain
    return jnp.minimum(jnp.maximum(result, -bound), bound).astype(held_as)


def setup_inputs(seed: int = 0) -> dict:
    splits = jax.random.split(jax.random.key(seed), 12)
    return {
        "psi_start": bell_draw(splits[0], (PHASES, 2 * FIELDS, NA, NR, NT), 1.0, 6.0, ((0, 4), (2, 2), (3, 4)), jnp.float32),
        "source": bell_draw(splits[1], (PHASES, 2 * FIELDS, NA, NR, NT), 1.0, 6.0, ((0, 4), (2, 2), (3, 4)), jnp.float32),
        "face_coef": jnp.clip(jnp.exp(math.log(1.0) - 2.306499 * jax.random.uniform(splits[2], (6, NA, NR, NT), jnp.float32) ** block_scale(splits[2], (6, NA, NR, NT), ((1, 2), (2, 4)), -0.2, 0.2)), 0.099609375, 1.0).astype(jnp.bfloat16),
        "diag_coef": jnp.clip(6.0 + 4.0 * jax.random.uniform(splits[3], (NA, NR, NT), jnp.float32) ** block_scale(splits[3], (NA, NR, NT), ((0, 2), (1, 4)), -0.2, 0.2), 6.0, 10.0),
        "flux_jac": bell_draw(splits[4], (6, 2, FIELDS, FIELDS), (2 * FIELDS) ** -0.5, 2.0, (), jnp.float32),
        "omega": jnp.clip(jax.random.uniform(splits[5], (1,), jnp.float32, 0.5, 2.0), 0.5, 2.0),
        "metric": bell_draw(splits[6], (3, 2 * FIELDS), (2 * FIELDS) ** -0.5, 2.0, (), jnp.float32),
        "mode_shape": bell_draw(splits[7], (MODES, 3, NA, NR, NT), 1.0, 6.0, ((2, 2), (3, 4))),
        "phase_weight": jnp.clip(jnp.exp(math.log(0.5) - 2.3025851 * jax.random.uniform(splits[8], (PHASES,), jnp.float32) ** block_scale(splits[8], (PHASES,), ((0, 4),), -0.2, 0.2)), 0.05, 0.5),
        "pairing": jax.vmap(lambda own: jax.random.permutation(own, FACE))(jax.random.split(splits[9], N_AXIAL * N_RADIAL)).reshape((N_AXIAL, N_RADIAL, FACE)).astype(jnp.int32),
        "owner_order": jax.vmap(lambda own: jax.random.permutation(own, CELLS))(jax.random.split(splits[10], N_AXIAL * N_RADIAL)).reshape((N_AXIAL, N_RADIAL, CELLS)).astype(jnp.int32),
    }


RELAX = 0.8


def build_matrices(flux_jac):
    real_part = jnp.swapaxes(flux_jac[:, 0], 1, 2)
    imag_part = jnp.swapaxes(flux_jac[:, 1], 1, 2)
    top_rows = jnp.concatenate([real_part, imag_part], axis=2)
    low_rows = jnp.concatenate([-imag_part, real_part], axis=2)
    return jnp.concatenate([top_rows, low_rows], axis=1)


def rotate(values, angle):
    shape = (-1,) + (1,) * (values.ndim - 1)
    cosine = jnp.cos(angle).reshape(shape)
    sine = jnp.sin(angle).reshape(shape)
    half = values.shape[1] // 2
    real_part = values[:, :half]
    imag_part = values[:, half:]
    return jnp.concatenate([cosine * real_part - sine * imag_part, sine * real_part + cosine * imag_part], axis=1)


def pair_face(face, pairing):
    phases, comps, total_a, total_r = face.shape
    n_ax, n_ra, face_n = pairing.shape
    tile_a = total_a // n_ax
    tile_r = total_r // n_ra
    tiles = face.reshape(phases, comps, n_ax, tile_a, n_ra, tile_r).transpose(0, 1, 2, 4, 3, 5)
    tiles = tiles.reshape(phases, comps, n_ax, n_ra, tile_a * tile_r)
    index = jnp.broadcast_to(pairing.astype(jnp.int32)[None, None], tiles.shape)
    picked = jnp.take_along_axis(tiles, index, axis=4)
    picked = picked.reshape(phases, comps, n_ax, n_ra, tile_a, tile_r).transpose(0, 1, 2, 4, 3, 5)
    return picked.reshape(phases, comps, total_a, total_r)


def reference(psi_start, source, face_coef, diag_coef, flux_jac, omega, metric, mode_shape, phase_weight, pairing, owner_order):
    matrices = build_matrices(flux_jac)
    coef = face_coef.astype(jnp.float32)
    phases = psi_start.shape[0]
    angle = jnp.arange(phases).astype(jnp.float32) * (2.0 * math.pi / BLADES)
    half = psi_start.shape[1] // 2
    psi = psi_start
    for section in range(ITERS):
        parts = []
        for direction in range(6):
            applied = jnp.einsum("xc,pcart->pxart", matrices[direction], psi, precision=lax.Precision.HIGHEST)
            parts.append(applied * coef[direction][None, None])
        zero_a = jnp.zeros_like(parts[0][:, :, :1])
        zero_r = jnp.zeros_like(parts[0][:, :, :, :1])
        incoming = jnp.concatenate([zero_a, parts[0][:, :, :-1]], axis=2)
        incoming = incoming + jnp.concatenate([parts[1][:, :, 1:], zero_a], axis=2)
        incoming = incoming + jnp.concatenate([zero_r, parts[2][:, :, :, :-1]], axis=3)
        incoming = incoming + jnp.concatenate([parts[3][:, :, :, 1:], zero_r], axis=3)
        plus_wrap = rotate(pair_face(parts[4][..., -1], pairing), angle)
        minus_wrap = rotate(pair_face(parts[5][..., 0], pairing), -angle)
        incoming = incoming + jnp.concatenate([plus_wrap[..., None], parts[4][..., :-1]], axis=4)
        incoming = incoming + jnp.concatenate([parts[5][..., 1:], minus_wrap[..., None]], axis=4)
        swapped = jnp.concatenate([psi[:, half:], -psi[:, :half]], axis=1)
        residual = source - (diag_coef * psi + omega[0] * swapped) + incoming
        psi = psi + RELAX * residual / diag_coef
    heights = jnp.einsum("dc,pcart->pdart", metric, psi, precision=lax.Precision.HIGHEST)
    weighted = jnp.sum(phase_weight[:, None, None, None, None] * heights, axis=0)
    modes = mode_shape.astype(jnp.float32)
    total = modes[:, 0] * weighted[0] + modes[:, 1] * weighted[1] + modes[:, 2] * weighted[2]
    n_ax, n_ra, cells = owner_order.shape
    count_k, total_a, total_r, pitch = total.shape
    tile_a = total_a // n_ax
    tile_r = total_r // n_ra
    tiles = total.reshape(count_k, n_ax, tile_a, n_ra, tile_r, pitch).transpose(0, 1, 3, 2, 4, 5)
    tiles = tiles.reshape(count_k, n_ax, n_ra, cells)
    index = jnp.broadcast_to(owner_order.astype(jnp.int32)[None], tiles.shape)
    sens = jnp.take_along_axis(tiles, index, axis=3)
    return psi, sens
```

```python
import functools
import math

import jax
import jax.numpy as jnp
from jax import lax
from jax.experimental import pallas as pl
from jax.experimental.pallas import tpu as pltpu
from jax.sharding import PartitionSpec as P

BLADES = 16
ITERS = 4
RELAX = 0.8
MESH = pl.DeviceIdType.MESH
TILE = 256
TOP = 8


def kernel(
    sizes,
    psi_ref,
    source_ref,
    face_ref,
    diag_ref,
    flux_ref,
    omega_ref,
    metric_ref,
    mode_ref,
    weight_ref,
    pairing_ref,
    owner_ref,
    out_ref,
    sens_ref,
    psi,
    axial_low,
    axial_high,
    radial_sent,
    radial_low,
    radial_high,
    face_sent,
    face_low,
    face_high,
    coef,
    acc,
    inverse,
    wrapped,
    pair_matrix,
    one_hot,
    row_mask,
    modes_owned,
    weighted,
    gathered,
    received,
    matrix,
    send_sem,
    recv_sem,
    face_send_sem,
    face_recv_sem,
    phase_send_sem,
    phase_recv_sem,
):
    n_phase, n_axial, n_radial = sizes
    comps, tile_a, tile_r, pitch = psi_ref.shape
    half = comps // 2
    nodes = tile_a * tile_r
    fold = nodes // 2
    n_tiles = owner_ref.shape[1] // TILE
    own_tiles = n_tiles // n_phase
    n_modes = mode_ref.shape[0]
    phase = lax.axis_index("phase")
    ax = lax.axis_index("axial")
    rad = lax.axis_index("radial")
    has_low = (ax > 0, rad > 0)
    has_high = (ax < n_axial - 1, rad < n_radial - 1)
    rows = pl.ds(TOP, tile_r)

    barrier = pltpu.get_barrier_semaphore()
    for k in range(1, n_phase):
        pl.semaphore_signal(
            barrier,
            inc=1,
            device_id={"phase": lax.rem(phase + k, n_phase)},
            device_id_type=MESH,
        )
    for name, me, low, high in (
        ("axial", ax, has_low[0], has_high[0]),
        ("radial", rad, has_low[1], has_high[1]),
    ):
        @pl.when(low)
        def _():
            pl.semaphore_signal(barrier, inc=1, device_id={name: me - 1}, device_id_type=MESH)

        @pl.when(high)
        def _():
            pl.semaphore_signal(barrier, inc=1, device_id={name: me + 1}, device_id_type=MESH)

    for a in range(tile_a):
        psi[0, a, :, TOP : TOP + tile_r, :] = psi_ref[:, a]
        for d in range(6):
            coef[d, a] = face_ref[d, a].astype(jnp.float32)
    for a in range(tile_a):
        face_sent[2, a : a + 1, :] = coef[2, a, tile_r - 1 : tile_r, :]
        face_sent[3, a : a + 1, :] = coef[3, a, 0:1, :]
    for r in range(tile_r // 4):
        face_sent[0, 4 * r : 4 * r + 4, :] = coef[0, tile_a - 1, 4 * r : 4 * r + 4, :]
        face_sent[1, 4 * r : 4 * r + 4, :] = coef[1, 0, 4 * r : 4 * r + 4, :]

    greeted = n_phase - 1 + sum(jnp.where(flag, 1, 0) for flag in has_low + has_high)
    pl.semaphore_wait(barrier, greeted)

    def axial_copy(s, up):
        return pltpu.make_async_remote_copy(
            src_ref=psi.at[s, tile_a - 1 if up else 0, :, rows, :],
            dst_ref=(axial_low if up else axial_high).at[s],
            send_sem=send_sem.at[s, 0 if up else 1],
            recv_sem=recv_sem.at[s, 0 if up else 1],
            device_id={"axial": ax + 1 if up else ax - 1},
            device_id_type=MESH,
        )

    def radial_copy(s, up):
        return pltpu.make_async_remote_copy(
            src_ref=radial_sent.at[s, 0 if up else 1],
            dst_ref=(radial_low if up else radial_high).at[s],
            send_sem=send_sem.at[s, 2 if up else 3],
            recv_sem=recv_sem.at[s, 2 if up else 3],
            device_id={"radial": rad + 1 if up else rad - 1},
            device_id_type=MESH,
        )

    def face_copy(d):
        name, me = ("axial", ax) if d < 2 else ("radial", rad)
        count = tile_r if d < 2 else tile_a
        up = d % 2 == 0
        return pltpu.make_async_remote_copy(
            src_ref=face_sent.at[d],
            dst_ref=(face_low if up else face_high).at[d // 2],
            send_sem=face_send_sem.at[d],
            recv_sem=face_recv_sem.at[d],
            device_id={name: me + 1 if up else me - 1},
            device_id_type=MESH,
        )

    def start_section(s):
        for up in (True, False):
            @pl.when((has_high if up else has_low)[0])
            def _():
                axial_copy(s, up).start()

        for a in range(tile_a):
            radial_sent[s, 0, :, a, :] = psi[s, a, :, TOP + tile_r - 1, :]
            radial_sent[s, 1, :, a, :] = psi[s, a, :, TOP, :]
        for up in (True, False):
            @pl.when((has_high if up else has_low)[1])
            def _():
                radial_copy(s, up).start()

    start_section(0)
    for d in range(6 - 2):
        @pl.when((has_high if d % 2 == 0 else has_low)[d // 2])
        def _():
            face_copy(d).start()

    for d in range(6):
        for j in range(half):
            for i in range(half):
                at = (d * half + j) * half + i
                real, imag = flux_ref[d, 0, j, i], flux_ref[d, 1, j, i]
                matrix[0, at] = real
                matrix[1, at] = real - imag
                matrix[2, at] = real + imag

    node = lax.broadcasted_iota(jnp.int32, (2 * nodes, nodes), 0)
    partner = jnp.where(node >= nodes, node - nodes, node) == pairing_ref[...]
    pair_matrix[...] = jnp.where(partner, 1.0, 0.0).T.astype(jnp.bfloat16)

    def permuted(value):
        high = value.astype(jnp.bfloat16)
        low = (value - high.astype(jnp.float32)).astype(jnp.bfloat16)
        stacked = jnp.concatenate([high, low], axis=0)
        return jnp.dot(pair_matrix[...], stacked, preferred_element_type=jnp.float32)

    lane = lax.broadcasted_iota(jnp.int32, (tile_r, pitch), 1)
    for d, from_lane in ((4, pitch - 1), (5, 0)):
        partner_face = permuted(coef[d].reshape(nodes, pitch))
        for a in range(tile_a):
            own = jnp.where(
                lane == from_lane, partner_face[a * tile_r : (a + 1) * tile_r], coef[d, a]
            )
            coef[d, a] = pltpu.roll(own, 1 if d == 4 else pitch - 1, 1)

    for a in range(tile_a):
        inverse[a] = RELAX / diag_ref[a]

    angle = 2.0 * math.pi / BLADES
    turn = lax.rem(phase, BLADES)
    cosine = jnp.float32(1.0)
    sine = jnp.float32(0.0)
    for k in range(1, BLADES):
        cosine = jnp.where(turn == k, jnp.float32(math.cos(angle * k)), cosine)
        sine = jnp.where(turn == k, jnp.float32(math.sin(angle * k)), sine)

    def make_one_hot(t, _):
        owner = owner_ref[:, pl.ds(pl.multiple_of(t * TILE, TILE), TILE)]
        row = lax.div(owner, pitch)
        column = owner - row * pitch
        later = row >= fold
        column = jnp.where(later, column + pitch, column)
        row = jnp.where(later, row - fold, row)
        at = lax.broadcasted_iota(jnp.int32, (2 * pitch, TILE), 0)
        one_hot[t] = jnp.where(at == column, 1.0, 0.0).astype(jnp.bfloat16)
        at = lax.broadcasted_iota(jnp.int32, (fold, TILE), 0)
        row_mask[t] = jnp.where(at == row, 1.0, 0.0)
        return 0

    lax.fori_loop(0, n_tiles, make_one_hot, 0)

    def gather_modes(i, _):
        t = phase * own_tiles + i
        for d in range(3):
            for k in range(0, n_modes, 6):
                part = mode_ref[k : k + 6, d].reshape(6, nodes, pitch)
                left = part[:, :fold].reshape(6 * fold, pitch)
                right = part[:, fold:].reshape(6 * fold, pitch)
                picked = jnp.dot(
                    jnp.concatenate([left, right], axis=1),
                    one_hot[t],
                    preferred_element_type=jnp.float32,
                )
                picked = picked.reshape(6, fold, TILE) * row_mask[t][None]
                modes_owned[i, d, k : k + 6, :] = jnp.sum(picked, axis=1)
        return 0

    def apply(d, values, totals):
        first, second, third = totals
        both = [values[j] + values[half + j] for j in range(half)]
        for i in range(half):
            for j in range(half):
                at = (d * half + j) * half + i
                first[i] = first[i] + matrix[0, at] * both[j]
                second[i] = second[i] + matrix[1, at] * values[half + j]
                third[i] = third[i] + matrix[2, at] * values[j]
        return totals

    def read(a):
        return [[acc[k, a, i] for i in range(half)] for k in range(3)]

    def write(a, totals):
        for k in range(3):
            for i in range(half):
                acc[k, a, i] = totals[k][i]

    def section(s, _):
        for c in range(comps):
            whole = psi[s, :, c, TOP : TOP + tile_r, :].reshape(nodes, pitch)
            wrapped[c] = permuted(whole).reshape(tile_a, tile_r, pitch)

        def pitch_part(a, _):
            zero = jnp.zeros((tile_r, pitch), jnp.float32)
            totals = [[zero] * half for _ in range(3)]
            for d, from_lane in ((4, pitch - 1), (5, 0)):
                sign = sine if d == 4 else -sine
                values = [None] * comps
                for j in range(half):
                    real, imag = wrapped[j, a], wrapped[half + j, a]
                    turned = (cosine * real - sign * imag, sign * real + cosine * imag)
                    for c, value in ((j, turned[0]), (half + j, turned[1])):
                        value = jnp.where(
                            lane == from_lane, value, psi[s, a, c, TOP : TOP + tile_r, :]
                        )
                        value = pltpu.roll(value, 1 if d == 4 else pitch - 1, 1)
                        values[c] = coef[d, a] * value
                totals = apply(d, values, totals)
            write(a, totals)
            return 0

        lax.fori_loop(0, tile_a, pitch_part, 0)

        def inner_axial(a, _):
            up = [coef[0, a] * psi[s, a, c, TOP : TOP + tile_r, :] for c in range(comps)]
            write(a + 1, apply(0, up, read(a + 1)))
            down = [
                coef[1, a + 1] * psi[s, a + 1, c, TOP : TOP + tile_r, :] for c in range(comps)
            ]
            write(a, apply(1, down, read(a)))
            return 0

        lax.fori_loop(0, tile_a - 1, inner_axial, 0)
        lax.fori_loop(
            lax.div(own_tiles * s, ITERS), lax.div(own_tiles * (s + 1), ITERS), gather_modes, 0
        )

        for up in (True, False):
            flag = (has_low if up else has_high)[1]
            at = TOP - 1 if up else TOP + tile_r
            got = radial_low if up else radial_high

            @pl.when(flag)
            def _():
                radial_copy(s, up).wait_recv()
                for a in range(tile_a):
                    psi[s, a, :, at, :] = got[s, :, a, :]

            @pl.when(jnp.logical_not(flag))
            def _():
                for a in range(tile_a):
                    psi[s, a, :, at, :] = jnp.zeros((comps, pitch), jnp.float32)

        @pl.when(s == 0)
        def _():
            for d in (2, 3):
                flag = (has_low if d == 2 else has_high)[1]
                got = face_low if d == 2 else face_high

                @pl.when(flag)
                def _():
                    face_copy(d).wait_recv()

                row = lax.broadcasted_iota(jnp.int32, (tile_r, pitch), 0)
                edge = 0 if d == 2 else tile_r - 1
                for a in range(tile_a):
                    moved = pltpu.roll(coef[d, a], 1 if d == 2 else tile_r - 1, 0)
                    coef[d, a] = jnp.where(row == edge, 0.0, moved)

                @pl.when(flag)
                def _():
                    for a in range(tile_a):
                        coef[d, a, edge : edge + 1, :] = got[1, a : a + 1, :]

        def radial_part(a, _):
            totals = read(a)
            for d, at in ((2, TOP - 1), (3, TOP + 1)):
                values = [coef[d, a] * psi[s, a, c, at : at + tile_r, :] for c in range(comps)]
                totals = apply(d, values, totals)
            write(a, totals)
            return 0

        lax.fori_loop(0, tile_a, radial_part, 0)

        for up in (True, False):
            @pl.when((has_low if up else has_high)[0])
            def _():
                @pl.when(s == 0)
                def _():
                    face_copy(0 if up else 1).wait_recv()

                axial_copy(s, up).wait_recv()
                got = axial_low if up else axial_high
                weight = (face_low if up else face_high)[0]
                a = 0 if up else tile_a - 1
                values = [weight * got[s, c] for c in range(comps)]
                write(a, apply(0 if up else 1, values, read(a)))

        omega = omega_ref[0]

        def update(a, _):
            first, second, third = read(a)
            scale = inverse[a]
            for i in range(half):
                real = psi[s, a, i, TOP : TOP + tile_r, :]
                imag = psi[s, a, half + i, TOP : TOP + tile_r, :]
                got_real = source_ref[i, a] - omega * imag + (first[i] - second[i])
                got_imag = source_ref[half + i, a] + omega * real + (first[i] - third[i])
                psi[s + 1, a, i, TOP : TOP + tile_r, :] = (1.0 - RELAX) * real + scale * got_real
                psi[s + 1, a, half + i, TOP : TOP + tile_r, :] = (
                    1.0 - RELAX
                ) * imag + scale * got_imag
            return 0

        lax.fori_loop(0, tile_a, update, 0)

        @pl.when(s + 1 < ITERS)
        def _():
            start_section(s + 1)

        return 0

    lax.fori_loop(0, ITERS, section, 0)

    share = weight_ref[0]
    for a in range(tile_a):
        values = [psi[ITERS, a, c, TOP : TOP + tile_r, :] for c in range(comps)]
        row = (a * tile_r) % fold
        column = pitch * ((a * tile_r) // fold)
        for d in range(3):
            height = metric_ref[d, 0] * values[0]
            for c in range(1, comps):
                height = height + metric_ref[d, c] * values[c]
            height = share * height
            high = height.astype(jnp.bfloat16)
            low = (height - high.astype(jnp.float32)).astype(jnp.bfloat16)
            for part, value in ((0, high), (1, low)):
                at = (part * 3 + d) * fold + row
                weighted[at : at + tile_r, column : column + pitch] = value

    def gather_weighted(t, _):
        picked = jnp.dot(weighted[...], one_hot[t], preferred_element_type=jnp.float32)
        picked = picked.reshape(2, 3, fold, TILE)
        gathered[t] = jnp.sum((picked[0] + picked[1]) * row_mask[t][None], axis=1)
        return 0

    def phase_copy(k):
        peer = lax.rem(phase + k, n_phase)
        return pltpu.make_async_remote_copy(
            src_ref=gathered.at[pl.ds(peer * own_tiles, own_tiles)],
            dst_ref=received.at[k],
            send_sem=phase_send_sem.at[k],
            recv_sem=phase_recv_sem.at[k],
            device_id={"phase": peer},
            device_id_type=MESH,
        )

    for k in list(range(1, n_phase)) + [0]:
        peer = lax.rem(phase + k, n_phase)
        lax.fori_loop(peer * own_tiles, (peer + 1) * own_tiles, gather_weighted, 0)
        if k:
            phase_copy(k).start()

    for a in range(tile_a):
        out_ref[:, a] = psi[ITERS, a, :, TOP : TOP + tile_r, :]

    for k in range(1, n_phase):
        phase_copy(k).wait_recv()

    for i in range(own_tiles):
        total = gathered[phase * own_tiles + i]
        for k in range(1, n_phase):
            total = total + received[k, i]
        result = modes_owned[i, 0] * total[0:1]
        for d in range(1, 3):
            result = result + modes_owned[i, d] * total[d : d + 1]
        sens_ref[:, i * TILE : (i + 1) * TILE] = result

    for k in range(1, n_phase):
        phase_copy(k).wait_send()
    for up in (True, False):
        flags = has_high if up else has_low

        @pl.when(flags[0])
        def _():
            face_copy(0 if up else 1).wait_send()
            for s in range(ITERS):
                axial_copy(s, up).wait_send()

        @pl.when(flags[1])
        def _():
            face_copy(2 if up else 3).wait_send()
            for s in range(ITERS):
                radial_copy(s, up).wait_send()


def body(
    sizes,
    psi_start,
    source,
    face_coef,
    diag_coef,
    flux_jac,
    omega,
    metric,
    mode_shape,
    phase_weight,
    pairing,
    owner_order,
):
    _, comps, tile_a, tile_r, pitch = psi_start.shape
    half = comps // 2
    nodes = tile_a * tile_r
    cells = nodes * pitch
    n_phase = sizes[0]
    n_tiles = cells // TILE
    own_tiles = n_tiles // n_phase
    owned = cells // n_phase
    count_k = mode_shape.shape[0]
    f32, bf16 = jnp.float32, jnp.bfloat16
    vmem = pl.BlockSpec(memory_space=pltpu.VMEM)
    smem = pl.BlockSpec(memory_space=pltpu.SMEM)
    dma = pltpu.SemaphoreType.DMA
    psi_out, sens = pl.pallas_call(
        functools.partial(kernel, sizes),
        out_shape=(
            jax.ShapeDtypeStruct((comps, tile_a, tile_r, pitch), f32),
            jax.ShapeDtypeStruct((count_k, owned), f32),
        ),
        in_specs=[vmem, vmem, vmem, vmem, smem, smem, smem, vmem, smem, vmem, vmem],
        out_specs=(vmem, vmem),
        scratch_shapes=[
            pltpu.VMEM((ITERS + 1, tile_a, comps, tile_r + 2 * TOP, pitch), f32),
            pltpu.VMEM((ITERS, comps, tile_r, pitch), f32),
            pltpu.VMEM((ITERS, comps, tile_r, pitch), f32),
            pltpu.VMEM((ITERS, 2, comps, tile_a, pitch), f32),
            pltpu.VMEM((ITERS, comps, tile_a, pitch), f32),
            pltpu.VMEM((ITERS, comps, tile_a, pitch), f32),
            pltpu.VMEM((4, tile_r, pitch), f32),
            pltpu.VMEM((2, tile_r, pitch), f32),
            pltpu.VMEM((2, tile_r, pitch), f32),
            pltpu.VMEM((6, tile_a, tile_r, pitch), f32),
            pltpu.VMEM((3, tile_a, half, tile_r, pitch), f32),
            pltpu.VMEM((tile_a, tile_r, pitch), f32),
            pltpu.VMEM((comps, tile_a, tile_r, pitch), f32),
            pltpu.VMEM((nodes, 2 * nodes), bf16),
            pltpu.VMEM((n_tiles, 2 * pitch, TILE), bf16),
            pltpu.VMEM((n_tiles, nodes // 2, TILE), f32),
            pltpu.VMEM((own_tiles, 3, count_k, TILE), f32),
            pltpu.VMEM((3 * nodes, 2 * pitch), bf16),
            pltpu.VMEM((n_tiles, 3, TILE), f32),
            pltpu.VMEM((n_phase, own_tiles, 3, TILE), f32),
            pltpu.SMEM((3, 6 * half * half), f32),
            dma((ITERS, 4)),
            dma((ITERS, 4)),
            dma((4,)),
            dma((4,)),
            dma((n_phase,)),
            dma((n_phase,)),
        ],
        compiler_params=pltpu.CompilerParams(
            collective_id=0, has_side_effects=True, vmem_limit_bytes=48 * 1024 * 1024
        ),
    )(
        psi_start[0],
        source[0],
        face_coef,
        diag_coef,
        flux_jac,
        omega,
        metric,
        mode_shape,
        phase_weight,
        pairing[0],
        owner_order[0],
    )
    return (psi_out[None], sens.reshape(count_k, 1, 1, owned))


def solution(mesh):
    sizes = tuple(mesh.shape[name] for name in ("phase", "axial", "radial"))
    return jax.shard_map(
        functools.partial(body, sizes),
        mesh=mesh,
        in_specs=(
            P("phase", None, "axial", "radial", None),
            P("phase", None, "axial", "radial", None),
            P(None, "axial", "radial", None),
            P("axial", "radial", None),
            P(),
            P(),
            P(),
            P(None, None, "axial", "radial", None),
            P("phase"),
            P("axial", "radial", None),
            P("axial", "radial", None),
        ),
        out_specs=(P("phase", None, "axial", "radial", None), P(None, "axial", "radial", "phase")),
        check_vma=False,
    )
```

```python
import functools
import math

import jax
import jax.numpy as jnp
from jax import lax
from jax.experimental import pallas as pl
from jax.experimental.pallas import tpu as pltpu
from jax.sharding import PartitionSpec as P

BLADES = 16
ITERS = 4
RELAX = 0.8
MESH = pl.DeviceIdType.MESH
TILE = 256
TOP = 8


def split(value):
    high = value.astype(jnp.bfloat16)
    return high, (value - high.astype(jnp.float32)).astype(jnp.bfloat16)


def kernel(
    sizes,
    psi_in,
    source_in,
    face_in,
    diag_in,
    flux_in,
    omega_ref,
    metric_ref,
    mode_in,
    weight_ref,
    pairing_in,
    owner_in,
    out_ref,
    sens_ref,
    psi,
    source_ref,
    face_ref,
    diag_ref,
    flux_ref,
    mode_ref,
    pairing_ref,
    owner_ref,
    radial_sent,
    radial_low,
    radial_high,
    face_sent,
    face_low,
    face_high,
    coef,
    inverse,
    wrapped,
    pair_matrix,
    matrix,
    field_high,
    field_low,
    one_hot,
    row_mask,
    modes_owned,
    weighted,
    gathered,
    received,
    load_sem,
    send_sem,
    recv_sem,
    face_send_sem,
    face_recv_sem,
    phase_send_sem,
    phase_recv_sem,
):
    n_phase, n_axial, n_radial = sizes
    comps, tile_a, tile_r, pitch = source_ref.shape
    half = comps // 2
    nodes = tile_a * tile_r
    fold = nodes // 2
    n_tiles = owner_ref.shape[1] // TILE
    own_tiles = n_tiles // n_phase
    n_modes = mode_ref.shape[0]
    depth = 6 * comps * TOP
    phase = lax.axis_index("phase")
    ax = lax.axis_index("axial")
    rad = lax.axis_index("radial")
    has_low = (ax > 0, rad > 0)
    has_high = (ax < n_axial - 1, rad < n_radial - 1)
    rows = pl.ds(TOP, tile_r)

    loads = [
        pltpu.make_async_copy(psi_in.at[:, a], psi.at[0, a + 1, :, rows, :], load_sem.at[a])
        for a in range(tile_a)
    ]
    for pair in (
        (face_in, face_ref),
        (flux_in, flux_ref),
        (pairing_in, pairing_ref),
        (diag_in, diag_ref),
        (owner_in, owner_ref),
        (source_in, source_ref),
        (mode_in, mode_ref),
    ):
        loads.append(pltpu.make_async_copy(pair[0], pair[1], load_sem.at[len(loads)]))
    for copy in loads:
        copy.start()

    barrier = pltpu.get_barrier_semaphore()
    for k in range(1, n_phase):
        pl.semaphore_signal(
            barrier,
            inc=1,
            device_id={"phase": lax.rem(phase + k, n_phase)},
            device_id_type=MESH,
        )
    for name, me, low, high in (
        ("axial", ax, has_low[0], has_high[0]),
        ("radial", rad, has_low[1], has_high[1]),
    ):
        @pl.when(low)
        def _():
            pl.semaphore_signal(barrier, inc=1, device_id={name: me - 1}, device_id_type=MESH)

        @pl.when(high)
        def _():
            pl.semaphore_signal(barrier, inc=1, device_id={name: me + 1}, device_id_type=MESH)

    for flag, at, d in ((has_low[0], 0, 0), (has_high[0], tile_a + 1, 1)):
        @pl.when(jnp.logical_not(flag))
        def _():
            coef[d, at] = jnp.zeros((tile_r, pitch), jnp.float32)
            for s in range(ITERS):
                for c in range(comps):
                    psi[s, at, c, TOP : TOP + tile_r, :] = jnp.zeros(
                        (tile_r, pitch), jnp.float32
                    )

    def axial_copy(s, up):
        return pltpu.make_async_remote_copy(
            src_ref=psi.at[s, tile_a if up else 1, :, rows, :],
            dst_ref=psi.at[s, 0 if up else tile_a + 1, :, rows, :],
            send_sem=send_sem.at[s, 0 if up else 1],
            recv_sem=recv_sem.at[s, 0 if up else 1],
            device_id={"axial": ax + 1 if up else ax - 1},
            device_id_type=MESH,
        )

    def radial_copy(s, up):
        return pltpu.make_async_remote_copy(
            src_ref=radial_sent.at[s, 0 if up else 1],
            dst_ref=(radial_low if up else radial_high).at[s],
            send_sem=send_sem.at[s, 2 if up else 3],
            recv_sem=recv_sem.at[s, 2 if up else 3],
            device_id={"radial": rad + 1 if up else rad - 1},
            device_id_type=MESH,
        )

    def face_copy(d):
        up = d % 2 == 0
        if d < 2:
            src = coef.at[d, tile_a if up else 1]
            dst = coef.at[d, 0 if up else tile_a + 1]
            target = {"axial": ax + 1 if up else ax - 1}
        else:
            src = face_sent.at[d - 2]
            dst = face_low if up else face_high
            target = {"radial": rad + 1 if up else rad - 1}
        return pltpu.make_async_remote_copy(
            src_ref=src,
            dst_ref=dst,
            send_sem=face_send_sem.at[d],
            recv_sem=face_recv_sem.at[d],
            device_id=target,
            device_id_type=MESH,
        )

    def start_axial(s):
        for up in (True, False):
            @pl.when((has_high if up else has_low)[0])
            def _():
                axial_copy(s, up).start()

    def start_radial(s):
        for a in range(tile_a):
            radial_sent[s, 0, :, a, :] = psi[s, a + 1, :, TOP + tile_r - 1, :]
            radial_sent[s, 1, :, a, :] = psi[s, a + 1, :, TOP, :]
        for up in (True, False):
            @pl.when((has_high if up else has_low)[1])
            def _():
                radial_copy(s, up).start()

    for copy in loads[:tile_a]:
        copy.wait()
    greeted = n_phase - 1 + sum(jnp.where(flag, 1, 0) for flag in has_low + has_high)
    pl.semaphore_wait(barrier, greeted)
    start_axial(0)
    start_radial(0)

    loads[tile_a].wait()
    for a in range(tile_a):
        for d in range(6):
            coef[d, a + 1] = face_ref[d, a].astype(jnp.float32)
    for a in range(tile_a):
        face_sent[0, a : a + 1, :] = coef[2, a + 1, tile_r - 1 : tile_r, :]
        face_sent[1, a : a + 1, :] = coef[3, a + 1, 0:1, :]
    for d in range(4):
        @pl.when((has_high if d % 2 == 0 else has_low)[d // 2])
        def _():
            face_copy(d).start()

    loads[tile_a + 1].wait()
    real = [flux_ref[j, :, 0, :] for j in range(half)]
    imag = [flux_ref[j, :, 1, :] for j in range(half)]
    fine = lax.Precision.HIGHEST
    entries = (
        jnp.concatenate(real + imag, axis=1),
        jnp.concatenate([-value for value in imag] + real, axis=1),
    )
    tall, wide = comps * TOP, matrix.shape[1]
    spread = jnp.zeros((tall, 6 * comps), jnp.float32)
    row = lax.div(lax.broadcasted_iota(jnp.int32, (tall, half), 0), TOP)
    column = lax.broadcasted_iota(jnp.int32, (tall, half), 1)
    for k in range(2):
        pick = jnp.where(row == column + k * half, 1.0, 0.0)
        spread = spread + jnp.dot(
            pick, entries[k], precision=fine, preferred_element_type=jnp.float32
        )
    row = lax.broadcasted_iota(jnp.int32, (6 * comps, wide), 0)
    column = lax.div(lax.broadcasted_iota(jnp.int32, (6 * comps, wide), 1), TOP)
    spread = jnp.dot(
        spread,
        jnp.where(row == column, 1.0, 0.0),
        precision=fine,
        preferred_element_type=jnp.float32,
    )
    row = lax.rem(lax.broadcasted_iota(jnp.int32, (tall, wide), 0), TOP)
    column = lax.rem(lax.broadcasted_iota(jnp.int32, (tall, wide), 1), TOP)
    high, low = split(jnp.where(row == column, spread, 0.0))
    matrix[:tall] = high
    matrix[tall:] = low
    for slot in range(tile_a):
        for field in (field_high, field_low):
            field[slot, depth:, :] = jnp.zeros((wide - depth, 2 * pitch), jnp.bfloat16)

    loads[tile_a + 2].wait()
    node = lax.broadcasted_iota(jnp.int32, (2 * nodes, nodes), 0)
    partner = jnp.where(node >= nodes, node - nodes, node) == pairing_ref[...]
    pair_matrix[...] = jnp.where(partner, 1.0, 0.0).T.astype(jnp.bfloat16)

    def permuted(value):
        stacked = jnp.concatenate(split(value), axis=0)
        return jnp.dot(pair_matrix[...], stacked, preferred_element_type=jnp.float32)

    lane = lax.broadcasted_iota(jnp.int32, (tile_r, pitch), 1)
    for d, from_lane in ((4, pitch - 1), (5, 0)):
        partner_face = permuted(coef[d, 1 : tile_a + 1].reshape(nodes, pitch))
        for a in range(tile_a):
            own = jnp.where(
                lane == from_lane, partner_face[a * tile_r : (a + 1) * tile_r], coef[d, a + 1]
            )
            coef[d, a + 1] = pltpu.roll(own, 1 if d == 4 else pitch - 1, 1)

    loads[tile_a + 3].wait()
    for a in range(tile_a):
        inverse[a] = RELAX / diag_ref[a]

    angle = 2.0 * math.pi / BLADES
    turn = lax.rem(phase, BLADES)
    cosine = jnp.float32(1.0)
    sine = jnp.float32(0.0)
    for k in range(1, BLADES):
        cosine = jnp.where(turn == k, jnp.float32(math.cos(angle * k)), cosine)
        sine = jnp.where(turn == k, jnp.float32(math.sin(angle * k)), sine)

    def make_one_hot(u, _):
        t = lax.rem(phase * own_tiles + u, n_tiles)
        owner = owner_ref[:, pl.ds(pl.multiple_of(t * TILE, TILE), TILE)]
        row = lax.div(owner, pitch)
        column = owner - row * pitch
        later = row >= fold
        column = jnp.where(later, column + pitch, column)
        row = jnp.where(later, row - fold, row)
        at = lax.broadcasted_iota(jnp.int32, (2 * pitch, TILE), 0)
        one_hot[t] = jnp.where(at == column, 1.0, 0.0).astype(jnp.bfloat16)
        at = lax.broadcasted_iota(jnp.int32, (fold, TILE), 0)
        row_mask[t] = jnp.where(at == row, 1.0, 0.0)
        return 0

    def gather_modes(i, _):
        t = phase * own_tiles + i
        for d in range(3):
            for k in range(0, n_modes, 6):
                part = mode_ref[k : k + 6, d].reshape(6, nodes, pitch)
                left = part[:, :fold].reshape(6 * fold, pitch)
                right = part[:, fold:].reshape(6 * fold, pitch)
                picked = jnp.dot(
                    jnp.concatenate([left, right], axis=1),
                    one_hot[t],
                    preferred_element_type=jnp.float32,
                )
                picked = picked.reshape(6, fold, TILE) * row_mask[t][None]
                modes_owned[i, d, k : k + 6, :] = jnp.sum(picked, axis=1)
        return 0

    def build(s, a, slot):
        for c in range(comps):
            own = psi[s, a, c, TOP : TOP + tile_r, :]
            scaled = (
                coef[0, a - 1] * psi[s, a - 1, c, TOP : TOP + tile_r, :],
                coef[1, a + 1] * psi[s, a + 1, c, TOP : TOP + tile_r, :],
                coef[2, a] * psi[s, a, c, TOP - 1 : TOP + tile_r - 1, :],
                coef[3, a] * psi[s, a, c, TOP + 1 : TOP + tile_r + 1, :],
                coef[4, a] * pltpu.roll(jnp.where(lane == pitch - 1, wrapped[c, a - 1], own), 1, 1),
                coef[5, a]
                * pltpu.roll(jnp.where(lane == 0, wrapped[c, a - 1], own), pitch - 1, 1),
            )
            for d in range(0, 6, 2):
                at = (c * 6 + d) * TOP
                for k in range(2):
                    block = jnp.concatenate(
                        [value[k * TOP : (k + 1) * TOP] for value in scaled[d : d + 2]], axis=0
                    )
                    high, low = split(block)
                    columns = slice(k * pitch, (k + 1) * pitch)
                    field_high[slot, at : at + 2 * TOP, columns] = high
                    field_low[slot, at : at + 2 * TOP, columns] = low

    def update(s, a, slot):
        both = jnp.dot(matrix[...], field_high[slot], preferred_element_type=jnp.float32)
        rest = jnp.dot(matrix[:tall], field_low[slot], preferred_element_type=jnp.float32)
        total = both[:tall] + (both[tall:] + rest)
        omega = omega_ref[0]
        scale = inverse[a - 1]

        def incoming(c):
            part = total[c * TOP : (c + 1) * TOP]
            return jnp.concatenate([part[:, :pitch], part[:, pitch:]], axis=0)

        for i in range(half):
            real = psi[s, a, i, TOP : TOP + tile_r, :]
            imag = psi[s, a, half + i, TOP : TOP + tile_r, :]
            got_real = source_ref[i, a - 1] - omega * imag + incoming(i)
            got_imag = source_ref[half + i, a - 1] + omega * real + incoming(half + i)
            psi[s + 1, a, i, TOP : TOP + tile_r, :] = (1.0 - RELAX) * real + scale * got_real
            psi[s + 1, a, half + i, TOP : TOP + tile_r, :] = (
                1.0 - RELAX
            ) * imag + scale * got_imag

    def wait_axial(s):
        for up in (True, False):
            @pl.when((has_low if up else has_high)[0])
            def _():
                @pl.when(s == 0)
                def _():
                    face_copy(0 if up else 1).wait_recv()

                axial_copy(s, up).wait_recv()

    first = jnp.where(ax > 0, 2, 1)
    turned_sine = jnp.where(lane >= pitch // 2, sine, -sine)

    def section(s, _):
        for c in range(comps):
            whole = psi[s, 1 : tile_a + 1, c, TOP : TOP + tile_r, :].reshape(nodes, pitch)
            wrapped[c] = permuted(whole).reshape(tile_a, tile_r, pitch)
        for a in range(tile_a):
            for j in range(half):
                real, imag = wrapped[j, a], wrapped[half + j, a]
                wrapped[j, a] = cosine * real - turned_sine * imag
                wrapped[half + j, a] = turned_sine * real + cosine * imag

        @pl.when(s == 0)
        def _():
            for copy in loads[tile_a + 4 :]:
                copy.wait()

        lax.fori_loop(
            lax.div(n_tiles * s, ITERS), lax.div(n_tiles * (s + 1), ITERS), make_one_hot, 0
        )
        lax.fori_loop(
            lax.div(own_tiles * s, ITERS), lax.div(own_tiles * (s + 1), ITERS), gather_modes, 0
        )

        for up in (True, False):
            flag = (has_low if up else has_high)[1]
            at = TOP - 1 if up else TOP + tile_r
            got = radial_low if up else radial_high

            @pl.when(flag)
            def _():
                radial_copy(s, up).wait_recv()
                for a in range(tile_a):
                    psi[s, a + 1, :, at, :] = got[s, :, a, :]

            @pl.when(jnp.logical_not(flag))
            def _():
                for a in range(tile_a):
                    psi[s, a + 1, :, at, :] = jnp.zeros((comps, pitch), jnp.float32)

        @pl.when(s == 0)
        def _():
            for d in (2, 3):
                flag = (has_low if d == 2 else has_high)[1]
                got = face_low if d == 2 else face_high

                @pl.when(flag)
                def _():
                    face_copy(d).wait_recv()

                row = lax.broadcasted_iota(jnp.int32, (tile_r, pitch), 0)
                edge = 0 if d == 2 else tile_r - 1
                for a in range(tile_a):
                    moved = pltpu.roll(coef[d, a + 1], 1 if d == 2 else tile_r - 1, 0)
                    coef[d, a + 1] = jnp.where(row == edge, 0.0, moved)

                @pl.when(flag)
                def _():
                    for a in range(tile_a):
                        coef[d, a + 1, edge : edge + 1, :] = got[a : a + 1, :]

        if n_axial > 2:
            wait_axial(s)
        for k in range(tile_a - 1):
            build(s, first + k, k)
        for k in range(tile_a - 1):
            update(s, first + k, k)
        if n_axial <= 2:
            wait_axial(s)
        last = jnp.where(ax > 0, 1, tile_a)
        build(s, last, tile_a - 1)
        update(s, last, tile_a - 1)

        @pl.when(s + 1 < ITERS)
        def _():
            start_axial(s + 1)
            start_radial(s + 1)

        return 0

    lax.fori_loop(0, ITERS, section, 0)

    share = weight_ref[0]
    for a in range(tile_a):
        values = [psi[ITERS, a + 1, c, TOP : TOP + tile_r, :] for c in range(comps)]
        row = (a * tile_r) % fold
        column = pitch * ((a * tile_r) // fold)
        for d in range(3):
            height = metric_ref[d, 0] * values[0]
            for c in range(1, comps):
                height = height + metric_ref[d, c] * values[c]
            for part, value in enumerate(split(share * height)):
                at = (part * 3 + d) * fold + row
                weighted[at : at + tile_r, column : column + pitch] = value

    def gather_weighted(t):
        picked = jnp.dot(weighted[...], one_hot[t], preferred_element_type=jnp.float32)
        picked = picked.reshape(2, 3, fold, TILE)
        gathered[t] = jnp.sum((picked[0] + picked[1]) * row_mask[t][None], axis=1)

    def phase_copy(k):
        peer = lax.rem(phase + k, n_phase)
        return pltpu.make_async_remote_copy(
            src_ref=gathered.at[pl.ds(peer * own_tiles, own_tiles)],
            dst_ref=received.at[k],
            send_sem=phase_send_sem.at[k],
            recv_sem=phase_recv_sem.at[k],
            device_id={"phase": peer},
            device_id_type=MESH,
        )

    for k in list(range(1, n_phase)) + [0]:
        peer = lax.rem(phase + k, n_phase)
        for i in range(own_tiles):
            gather_weighted(peer * own_tiles + i)
        if k:
            phase_copy(k).start()

    for a in range(tile_a):
        out_ref[:, a] = psi[ITERS, a + 1, :, TOP : TOP + tile_r, :]

    for k in range(1, n_phase):
        phase_copy(k).wait_recv()

    for i in range(own_tiles):
        total = gathered[phase * own_tiles + i]
        for k in range(1, n_phase):
            total = total + received[k, i]
        result = modes_owned[i, 0] * total[0:1]
        for d in range(1, 3):
            result = result + modes_owned[i, d] * total[d : d + 1]
        sens_ref[:, i * TILE : (i + 1) * TILE] = result

    for k in range(1, n_phase):
        phase_copy(k).wait_send()
    for up in (True, False):
        flags = has_high if up else has_low

        @pl.when(flags[0])
        def _():
            face_copy(0 if up else 1).wait_send()
            for s in range(ITERS):
                axial_copy(s, up).wait_send()

        @pl.when(flags[1])
        def _():
            face_copy(2 if up else 3).wait_send()
            for s in range(ITERS):
                radial_copy(s, up).wait_send()


def body(
    sizes,
    psi_start,
    source,
    face_coef,
    diag_coef,
    flux_jac,
    omega,
    metric,
    mode_shape,
    phase_weight,
    pairing,
    owner_order,
):
    _, comps, tile_a, tile_r, pitch = psi_start.shape
    half = comps // 2
    nodes = tile_a * tile_r
    cells = nodes * pitch
    n_phase = sizes[0]
    n_tiles = cells // TILE
    own_tiles = n_tiles // n_phase
    owned = cells // n_phase
    count_k = mode_shape.shape[0]
    f32, bf16 = jnp.float32, jnp.bfloat16
    vmem = pl.BlockSpec(memory_space=pltpu.VMEM)
    smem = pl.BlockSpec(memory_space=pltpu.SMEM)
    hbm = pl.BlockSpec(memory_space=pltpu.HBM)
    dma = pltpu.SemaphoreType.DMA
    depth = -(-6 * comps * TOP // 128) * 128
    psi_out, sens = pl.pallas_call(
        functools.partial(kernel, sizes),
        out_shape=(
            jax.ShapeDtypeStruct((comps, tile_a, tile_r, pitch), f32),
            jax.ShapeDtypeStruct((count_k, owned), f32),
        ),
        in_specs=[hbm, hbm, hbm, hbm, hbm, smem, smem, hbm, smem, hbm, hbm],
        out_specs=(vmem, vmem),
        scratch_shapes=[
            pltpu.VMEM((ITERS + 1, tile_a + 2, comps, tile_r + 2 * TOP, pitch), f32),
            pltpu.VMEM((comps, tile_a, tile_r, pitch), f32),
            pltpu.VMEM((6, tile_a, tile_r, pitch), bf16),
            pltpu.VMEM((tile_a, tile_r, pitch), f32),
            pltpu.VMEM((half, half, 2, 6), f32),
            pltpu.VMEM((count_k, 3, tile_a, tile_r, pitch), bf16),
            pltpu.VMEM((1, nodes), jnp.int32),
            pltpu.VMEM((1, cells), jnp.int32),
            pltpu.VMEM((ITERS, 2, comps, tile_a, pitch), f32),
            pltpu.VMEM((ITERS, comps, tile_a, pitch), f32),
            pltpu.VMEM((ITERS, comps, tile_a, pitch), f32),
            pltpu.VMEM((2, tile_a, pitch), f32),
            pltpu.VMEM((tile_a, pitch), f32),
            pltpu.VMEM((tile_a, pitch), f32),
            pltpu.VMEM((6, tile_a + 2, tile_r, pitch), f32),
            pltpu.VMEM((tile_a, tile_r, pitch), f32),
            pltpu.VMEM((comps, tile_a, tile_r, pitch), f32),
            pltpu.VMEM((nodes, 2 * nodes), bf16),
            pltpu.VMEM((2 * comps * TOP, depth), bf16),
            pltpu.VMEM((tile_a, depth, 2 * pitch), bf16),
            pltpu.VMEM((tile_a, depth, 2 * pitch), bf16),
            pltpu.VMEM((n_tiles, 2 * pitch, TILE), bf16),
            pltpu.VMEM((n_tiles, nodes // 2, TILE), f32),
            pltpu.VMEM((own_tiles, 3, count_k, TILE), f32),
            pltpu.VMEM((3 * nodes, 2 * pitch), bf16),
            pltpu.VMEM((n_tiles, 3, TILE), f32),
            pltpu.VMEM((n_phase, own_tiles, 3, TILE), f32),
            dma((tile_a + 7,)),
            dma((ITERS, 4)),
            dma((ITERS, 4)),
            dma((4,)),
            dma((4,)),
            dma((n_phase,)),
            dma((n_phase,)),
        ],
        compiler_params=pltpu.CompilerParams(
            collective_id=0, has_side_effects=True, vmem_limit_bytes=48 * 1024 * 1024
        ),
    )(
        psi_start[0],
        source[0],
        face_coef,
        diag_coef,
        jnp.transpose(flux_jac, (2, 3, 1, 0)),
        omega,
        metric,
        mode_shape,
        phase_weight,
        pairing[0],
        owner_order[0],
    )
    return (psi_out[None], sens.reshape(count_k, 1, 1, owned))


def solution(mesh):
    sizes = tuple(mesh.shape[name] for name in ("phase", "axial", "radial"))
    return jax.shard_map(
        functools.partial(body, sizes),
        mesh=mesh,
        in_specs=(
            P("phase", None, "axial", "radial", None),
            P("phase", None, "axial", "radial", None),
            P(None, "axial", "radial", None),
            P("axial", "radial", None),
            P(),
            P(),
            P(),
            P(None, None, "axial", "radial", None),
            P("phase"),
            P("axial", "radial", None),
            P("axial", "radial", None),
        ),
        out_specs=(P("phase", None, "axial", "radial", None), P(None, "axial", "radial", "phase")),
        check_vma=False,
    )
```

```python
import functools
import math

import jax
import jax.numpy as jnp
from jax import lax
from jax.experimental import pallas as pl
from jax.experimental.pallas import tpu as pltpu
from jax.sharding import PartitionSpec as P

BLADES = 16
ITERS = 4
RELAX = 0.8
MESH = pl.DeviceIdType.MESH
TILE = 256
TOP = 8


def split(value):
    high = value.astype(jnp.bfloat16)
    return high, (value - high.astype(jnp.float32)).astype(jnp.bfloat16)


def kernel(
    sizes,
    psi_in,
    source_in,
    face_in,
    diag_in,
    flux_in,
    omega_ref,
    metric_ref,
    mode_in,
    weight_ref,
    pairing_in,
    owner_in,
    out_ref,
    sens_ref,
    psi,
    source_ref,
    face_ref,
    diag_ref,
    flux_ref,
    mode_ref,
    pairing_ref,
    owner_ref,
    radial_sent,
    radial_low,
    radial_high,
    face_sent,
    face_low,
    face_high,
    coef,
    inverse,
    wrapped,
    pair_matrix,
    matrix,
    field_high,
    field_low,
    one_hot,
    row_mask,
    modes_owned,
    weighted,
    gathered,
    received,
    load_sem,
    send_sem,
    recv_sem,
    face_send_sem,
    face_recv_sem,
    phase_send_sem,
    phase_recv_sem,
):
    n_phase, n_axial, n_radial = sizes
    comps, tile_a, tile_r, pitch = source_ref.shape
    half = comps // 2
    nodes = tile_a * tile_r
    fold = nodes // 2
    n_tiles = owner_ref.shape[1] // TILE
    own_tiles = n_tiles // n_phase
    n_modes = mode_ref.shape[0]
    depth = 6 * comps * TOP
    phase = lax.axis_index("phase")
    ax = lax.axis_index("axial")
    rad = lax.axis_index("radial")
    has_low = (ax > 0, rad > 0)
    has_high = (ax < n_axial - 1, rad < n_radial - 1)
    rows = pl.ds(TOP, tile_r)

    loads = [
        pltpu.make_async_copy(psi_in.at[:, a], psi.at[0, a + 1, :, rows, :], load_sem.at[a])
        for a in range(tile_a)
    ]
    for pair in (
        (face_in, face_ref),
        (flux_in, flux_ref),
        (pairing_in, pairing_ref),
        (diag_in, diag_ref),
        (owner_in, owner_ref),
        (source_in, source_ref),
        (mode_in, mode_ref),
    ):
        loads.append(pltpu.make_async_copy(pair[0], pair[1], load_sem.at[len(loads)]))
    for copy in loads:
        copy.start()

    barrier = pltpu.get_barrier_semaphore()
    for k in range(1, n_phase):
        pl.semaphore_signal(
            barrier,
            inc=1,
            device_id={"phase": lax.rem(phase + k, n_phase)},
            device_id_type=MESH,
        )
    for name, me, low, high in (
        ("axial", ax, has_low[0], has_high[0]),
        ("radial", rad, has_low[1], has_high[1]),
    ):
        @pl.when(low)
        def _():
            pl.semaphore_signal(barrier, inc=1, device_id={name: me - 1}, device_id_type=MESH)

        @pl.when(high)
        def _():
            pl.semaphore_signal(barrier, inc=1, device_id={name: me + 1}, device_id_type=MESH)

    for flag, at, d in ((has_low[0], 0, 0), (has_high[0], tile_a + 1, 1)):
        @pl.when(jnp.logical_not(flag))
        def _():
            coef[d, at] = jnp.zeros((tile_r, pitch), jnp.float32)
            for s in range(ITERS):
                for c in range(comps):
                    psi[s, at, c, TOP : TOP + tile_r, :] = jnp.zeros(
                        (tile_r, pitch), jnp.float32
                    )

    def axial_copy(s, up):
        return pltpu.make_async_remote_copy(
            src_ref=psi.at[s, tile_a if up else 1, :, rows, :],
            dst_ref=psi.at[s, 0 if up else tile_a + 1, :, rows, :],
            send_sem=send_sem.at[s, 0 if up else 1],
            recv_sem=recv_sem.at[s, 0 if up else 1],
            device_id={"axial": ax + 1 if up else ax - 1},
            device_id_type=MESH,
        )

    def radial_copy(s, up):
        return pltpu.make_async_remote_copy(
            src_ref=radial_sent.at[s, 0 if up else 1],
            dst_ref=(radial_low if up else radial_high).at[s],
            send_sem=send_sem.at[s, 2 if up else 3],
            recv_sem=recv_sem.at[s, 2 if up else 3],
            device_id={"radial": rad + 1 if up else rad - 1},
            device_id_type=MESH,
        )

    def face_copy(d):
        up = d % 2 == 0
        if d < 2:
            src = coef.at[d, tile_a if up else 1]
            dst = coef.at[d, 0 if up else tile_a + 1]
            target = {"axial": ax + 1 if up else ax - 1}
        else:
            src = face_sent.at[d - 2]
            dst = face_low if up else face_high
            target = {"radial": rad + 1 if up else rad - 1}
        return pltpu.make_async_remote_copy(
            src_ref=src,
            dst_ref=dst,
            send_sem=face_send_sem.at[d],
            recv_sem=face_recv_sem.at[d],
            device_id=target,
            device_id_type=MESH,
        )

    def start_axial(s):
        for up in (True, False):
            @pl.when((has_high if up else has_low)[0])
            def _():
                axial_copy(s, up).start()

    def start_radial(s):
        for a in range(tile_a):
            radial_sent[s, 0, :, a, :] = psi[s, a + 1, :, TOP + tile_r - 1, :]
            radial_sent[s, 1, :, a, :] = psi[s, a + 1, :, TOP, :]
        for up in (True, False):
            @pl.when((has_high if up else has_low)[1])
            def _():
                radial_copy(s, up).start()

    for copy in loads[:tile_a]:
        copy.wait()
    greeted = n_phase - 1 + sum(jnp.where(flag, 1, 0) for flag in has_low + has_high)
    pl.semaphore_wait(barrier, greeted)
    start_axial(0)
    start_radial(0)

    loads[tile_a].wait()
    for a in range(tile_a):
        for d in range(6):
            coef[d, a + 1] = face_ref[d, a].astype(jnp.float32)
    for a in range(tile_a):
        face_sent[0, a : a + 1, :] = coef[2, a + 1, tile_r - 1 : tile_r, :]
        face_sent[1, a : a + 1, :] = coef[3, a + 1, 0:1, :]
    for d in range(4):
        @pl.when((has_high if d % 2 == 0 else has_low)[d // 2])
        def _():
            face_copy(d).start()

    loads[tile_a + 1].wait()
    real = [flux_ref[j, :, 0, :] for j in range(half)]
    imag = [flux_ref[j, :, 1, :] for j in range(half)]
    fine = lax.Precision.HIGHEST
    entries = (
        jnp.concatenate(real + imag, axis=1),
        jnp.concatenate([-value for value in imag] + real, axis=1),
    )
    tall, wide = comps * TOP, matrix.shape[1]
    spread = jnp.zeros((tall, 6 * comps), jnp.float32)
    row = lax.div(lax.broadcasted_iota(jnp.int32, (tall, half), 0), TOP)
    column = lax.broadcasted_iota(jnp.int32, (tall, half), 1)
    for k in range(2):
        pick = jnp.where(row == column + k * half, 1.0, 0.0)
        spread = spread + jnp.dot(
            pick, entries[k], precision=fine, preferred_element_type=jnp.float32
        )
    row = lax.broadcasted_iota(jnp.int32, (6 * comps, wide), 0)
    column = lax.div(lax.broadcasted_iota(jnp.int32, (6 * comps, wide), 1), TOP)
    spread = jnp.dot(
        spread,
        jnp.where(row == column, 1.0, 0.0),
        precision=fine,
        preferred_element_type=jnp.float32,
    )
    row = lax.rem(lax.broadcasted_iota(jnp.int32, (tall, wide), 0), TOP)
    column = lax.rem(lax.broadcasted_iota(jnp.int32, (tall, wide), 1), TOP)
    high, low = split(jnp.where(row == column, spread, 0.0))
    matrix[:tall] = high
    matrix[tall:] = low
    for slot in range(tile_a):
        for field in (field_high, field_low):
            field[slot, depth:, :] = jnp.zeros((wide - depth, 2 * pitch), jnp.bfloat16)

    loads[tile_a + 2].wait()
    node = lax.broadcasted_iota(jnp.int32, (2 * nodes, nodes), 0)
    partner = jnp.where(node >= nodes, node - nodes, node) == pairing_ref[...]
    pair_matrix[...] = jnp.where(partner, 1.0, 0.0).T.astype(jnp.bfloat16)

    def permuted(value):
        stacked = jnp.concatenate(split(value), axis=0)
        return jnp.dot(pair_matrix[...], stacked, preferred_element_type=jnp.float32)

    lane = lax.broadcasted_iota(jnp.int32, (tile_r, pitch), 1)
    for d, from_lane in ((4, pitch - 1), (5, 0)):
        partner_face = permuted(coef[d, 1 : tile_a + 1].reshape(nodes, pitch))
        for a in range(tile_a):
            own = jnp.where(
                lane == from_lane, partner_face[a * tile_r : (a + 1) * tile_r], coef[d, a + 1]
            )
            coef[d, a + 1] = pltpu.roll(own, 1 if d == 4 else pitch - 1, 1)

    loads[tile_a + 3].wait()
    for a in range(tile_a):
        inverse[a] = RELAX / diag_ref[a]

    angle = 2.0 * math.pi / BLADES
    turn = lax.rem(phase, BLADES)
    cosine = jnp.float32(1.0)
    sine = jnp.float32(0.0)
    for k in range(1, BLADES):
        cosine = jnp.where(turn == k, jnp.float32(math.cos(angle * k)), cosine)
        sine = jnp.where(turn == k, jnp.float32(math.sin(angle * k)), sine)

    def make_one_hot(u, _):
        t = lax.rem(phase * own_tiles + u, n_tiles)
        owner = owner_ref[:, pl.ds(pl.multiple_of(t * TILE, TILE), TILE)]
        row = lax.div(owner, pitch)
        column = owner - row * pitch
        later = row >= fold
        column = jnp.where(later, column + pitch, column)
        row = jnp.where(later, row - fold, row)
        at = lax.broadcasted_iota(jnp.int32, (2 * pitch, TILE), 0)
        one_hot[t] = jnp.where(at == column, 1.0, 0.0).astype(jnp.bfloat16)
        at = lax.broadcasted_iota(jnp.int32, (fold, TILE), 0)
        row_mask[t] = jnp.where(at == row, 1.0, 0.0)
        return 0

    def gather_modes(i, _):
        t = phase * own_tiles + i
        for d in range(3):
            for k in range(0, n_modes, 6):
                part = mode_ref[k : k + 6, d].reshape(6, nodes, pitch)
                left = part[:, :fold].reshape(6 * fold, pitch)
                right = part[:, fold:].reshape(6 * fold, pitch)
                picked = jnp.dot(
                    jnp.concatenate([left, right], axis=1),
                    one_hot[t],
                    preferred_element_type=jnp.float32,
                )
                picked = picked.reshape(6, fold, TILE) * row_mask[t][None]
                modes_owned[i, d, k : k + 6, :] = jnp.sum(picked, axis=1)
        return 0

    def build(s, a, slot):
        for c in range(comps):
            own = psi[s, a, c, TOP : TOP + tile_r, :]
            scaled = (
                coef[0, a - 1] * psi[s, a - 1, c, TOP : TOP + tile_r, :],
                coef[1, a + 1] * psi[s, a + 1, c, TOP : TOP + tile_r, :],
                coef[2, a] * psi[s, a, c, TOP - 1 : TOP + tile_r - 1, :],
                coef[3, a] * psi[s, a, c, TOP + 1 : TOP + tile_r + 1, :],
                coef[4, a] * pltpu.roll(jnp.where(lane == pitch - 1, wrapped[c, a - 1], own), 1, 1),
                coef[5, a]
                * pltpu.roll(jnp.where(lane == 0, wrapped[c, a - 1], own), pitch - 1, 1),
            )
            for d in range(0, 6, 2):
                at = (c * 6 + d) * TOP
                for k in range(2):
                    block = jnp.concatenate(
                        [value[k * TOP : (k + 1) * TOP] for value in scaled[d : d + 2]], axis=0
                    )
                    high, low = split(block)
                    columns = slice(k * pitch, (k + 1) * pitch)
                    field_high[slot, at : at + 2 * TOP, columns] = high
                    field_low[slot, at : at + 2 * TOP, columns] = low

    def update(s, a, slot):
        both = jnp.dot(matrix[...], field_high[slot], preferred_element_type=jnp.float32)
        rest = jnp.dot(matrix[:tall], field_low[slot], preferred_element_type=jnp.float32)
        total = both[:tall] + (both[tall:] + rest)
        omega = omega_ref[0]
        scale = inverse[a - 1]

        def incoming(c):
            part = total[c * TOP : (c + 1) * TOP]
            return jnp.concatenate([part[:, :pitch], part[:, pitch:]], axis=0)

        for i in range(half):
            real = psi[s, a, i, TOP : TOP + tile_r, :]
            imag = psi[s, a, half + i, TOP : TOP + tile_r, :]
            got_real = source_ref[i, a - 1] - omega * imag + incoming(i)
            got_imag = source_ref[half + i, a - 1] + omega * real + incoming(half + i)
            psi[s + 1, a, i, TOP : TOP + tile_r, :] = (1.0 - RELAX) * real + scale * got_real
            psi[s + 1, a, half + i, TOP : TOP + tile_r, :] = (
                1.0 - RELAX
            ) * imag + scale * got_imag

    def wait_axial(s):
        for up in (True, False):
            @pl.when((has_low if up else has_high)[0])
            def _():
                @pl.when(s == 0)
                def _():
                    face_copy(0 if up else 1).wait_recv()

                axial_copy(s, up).wait_recv()

    first = jnp.where(ax > 0, 2, 1)
    turned_sine = jnp.where(lane >= pitch // 2, sine, -sine)

    def section(s, _):
        for c in range(comps):
            whole = psi[s, 1 : tile_a + 1, c, TOP : TOP + tile_r, :].reshape(nodes, pitch)
            wrapped[c] = permuted(whole).reshape(tile_a, tile_r, pitch)
        for a in range(tile_a):
            for j in range(half):
                real, imag = wrapped[j, a], wrapped[half + j, a]
                wrapped[j, a] = cosine * real - turned_sine * imag
                wrapped[half + j, a] = turned_sine * real + cosine * imag

        @pl.when(s == 0)
        def _():
            for copy in loads[tile_a + 4 :]:
                copy.wait()

        lax.fori_loop(
            lax.div(n_tiles * s, ITERS), lax.div(n_tiles * (s + 1), ITERS), make_one_hot, 0
        )
        lax.fori_loop(
            lax.div(own_tiles * s, ITERS), lax.div(own_tiles * (s + 1), ITERS), gather_modes, 0
        )

        for up in (True, False):
            flag = (has_low if up else has_high)[1]
            at = TOP - 1 if up else TOP + tile_r
            got = radial_low if up else radial_high

            @pl.when(flag)
            def _():
                radial_copy(s, up).wait_recv()
                for a in range(tile_a):
                    psi[s, a + 1, :, at, :] = got[s, :, a, :]

            @pl.when(jnp.logical_not(flag))
            def _():
                for a in range(tile_a):
                    psi[s, a + 1, :, at, :] = jnp.zeros((comps, pitch), jnp.float32)

        @pl.when(s == 0)
        def _():
            for d in (2, 3):
                flag = (has_low if d == 2 else has_high)[1]
                got = face_low if d == 2 else face_high

                @pl.when(flag)
                def _():
                    face_copy(d).wait_recv()

                row = lax.broadcasted_iota(jnp.int32, (tile_r, pitch), 0)
                edge = 0 if d == 2 else tile_r - 1
                for a in range(tile_a):
                    moved = pltpu.roll(coef[d, a + 1], 1 if d == 2 else tile_r - 1, 0)
                    coef[d, a + 1] = jnp.where(row == edge, 0.0, moved)

                @pl.when(flag)
                def _():
                    for a in range(tile_a):
                        coef[d, a + 1, edge : edge + 1, :] = got[a : a + 1, :]

        if n_axial > 2:
            wait_axial(s)
        for k in range(tile_a - 1):
            build(s, first + k, k)
        for k in range(tile_a - 1):
            update(s, first + k, k)
        if n_axial <= 2:
            wait_axial(s)
        last = jnp.where(ax > 0, 1, tile_a)
        build(s, last, tile_a - 1)
        update(s, last, tile_a - 1)

        @pl.when(s + 1 < ITERS)
        def _():
            start_axial(s + 1)
            start_radial(s + 1)

        return 0

    lax.fori_loop(0, ITERS, section, 0)

    share = weight_ref[0]
    for a in range(tile_a):
        values = [psi[ITERS, a + 1, c, TOP : TOP + tile_r, :] for c in range(comps)]
        row = (a * tile_r) % fold
        column = pitch * ((a * tile_r) // fold)
        for d in range(3):
            height = metric_ref[d, 0] * values[0]
            for c in range(1, comps):
                height = height + metric_ref[d, c] * values[c]
            for part, value in enumerate(split(share * height)):
                at = (part * 3 + d) * fold + row
                weighted[at : at + tile_r, column : column + pitch] = value

    def gather_weighted(t):
        picked = jnp.dot(weighted[...], one_hot[t], preferred_element_type=jnp.float32)
        picked = picked.reshape(2, 3, fold, TILE)
        gathered[t] = jnp.sum((picked[0] + picked[1]) * row_mask[t][None], axis=1)

    def phase_copy(k):
        peer = lax.rem(phase + k, n_phase)
        return pltpu.make_async_remote_copy(
            src_ref=gathered.at[pl.ds(peer * own_tiles, own_tiles)],
            dst_ref=received.at[k],
            send_sem=phase_send_sem.at[k],
            recv_sem=phase_recv_sem.at[k],
            device_id={"phase": peer},
            device_id_type=MESH,
        )

    for k in list(range(1, n_phase)) + [0]:
        peer = lax.rem(phase + k, n_phase)
        for i in range(own_tiles):
            gather_weighted(peer * own_tiles + i)
        if k:
            phase_copy(k).start()

    for a in range(tile_a):
        out_ref[:, a] = psi[ITERS, a + 1, :, TOP : TOP + tile_r, :]

    for k in range(1, n_phase):
        phase_copy(k).wait_recv()

    for i in range(own_tiles):
        total = gathered[phase * own_tiles + i]
        for k in range(1, n_phase):
            total = total + received[k, i]
        result = modes_owned[i, 0] * total[0:1]
        for d in range(1, 3):
            result = result + modes_owned[i, d] * total[d : d + 1]
        for k in range(TILE // pitch):
            sens_ref[:, i * (TILE // pitch) + k, :] = result[:, k * pitch : (k + 1) * pitch]

    for k in range(1, n_phase):
        phase_copy(k).wait_send()
    for up in (True, False):
        flags = has_high if up else has_low

        @pl.when(flags[0])
        def _():
            face_copy(0 if up else 1).wait_send()
            for s in range(ITERS):
                axial_copy(s, up).wait_send()

        @pl.when(flags[1])
        def _():
            face_copy(2 if up else 3).wait_send()
            for s in range(ITERS):
                radial_copy(s, up).wait_send()


def body(
    sizes,
    psi_start,
    source,
    face_coef,
    diag_coef,
    flux_jac,
    omega,
    metric,
    mode_shape,
    phase_weight,
    pairing,
    owner_order,
):
    _, comps, tile_a, tile_r, pitch = psi_start.shape
    half = comps // 2
    nodes = tile_a * tile_r
    cells = nodes * pitch
    n_phase = sizes[0]
    n_tiles = cells // TILE
    own_tiles = n_tiles // n_phase
    owned = cells // n_phase
    count_k = mode_shape.shape[0]
    f32, bf16 = jnp.float32, jnp.bfloat16
    vmem = pl.BlockSpec(memory_space=pltpu.VMEM)
    smem = pl.BlockSpec(memory_space=pltpu.SMEM)
    hbm = pl.BlockSpec(memory_space=pltpu.HBM)
    dma = pltpu.SemaphoreType.DMA
    depth = -(-6 * comps * TOP // 128) * 128
    psi_out, sens = pl.pallas_call(
        functools.partial(kernel, sizes),
        out_shape=(
            jax.ShapeDtypeStruct((comps, tile_a, tile_r, pitch), f32),
            jax.ShapeDtypeStruct((count_k, owned // pitch, pitch), f32),
        ),
        in_specs=[hbm, hbm, hbm, hbm, hbm, smem, smem, hbm, smem, hbm, hbm],
        out_specs=(vmem, vmem),
        scratch_shapes=[
            pltpu.VMEM((ITERS + 1, tile_a + 2, comps, tile_r + 2 * TOP, pitch), f32),
            pltpu.VMEM((comps, tile_a, tile_r, pitch), f32),
            pltpu.VMEM((6, tile_a, tile_r, pitch), bf16),
            pltpu.VMEM((tile_a, tile_r, pitch), f32),
            pltpu.VMEM((half, half, 2, 6), f32),
            pltpu.VMEM((count_k, 3, tile_a, tile_r, pitch), bf16),
            pltpu.VMEM((1, nodes), jnp.int32),
            pltpu.VMEM((1, cells), jnp.int32),
            pltpu.VMEM((ITERS, 2, comps, tile_a, pitch), f32),
            pltpu.VMEM((ITERS, comps, tile_a, pitch), f32),
            pltpu.VMEM((ITERS, comps, tile_a, pitch), f32),
            pltpu.VMEM((2, tile_a, pitch), f32),
            pltpu.VMEM((tile_a, pitch), f32),
            pltpu.VMEM((tile_a, pitch), f32),
            pltpu.VMEM((6, tile_a + 2, tile_r, pitch), f32),
            pltpu.VMEM((tile_a, tile_r, pitch), f32),
            pltpu.VMEM((comps, tile_a, tile_r, pitch), f32),
            pltpu.VMEM((nodes, 2 * nodes), bf16),
            pltpu.VMEM((2 * comps * TOP, depth), bf16),
            pltpu.VMEM((tile_a, depth, 2 * pitch), bf16),
            pltpu.VMEM((tile_a, depth, 2 * pitch), bf16),
            pltpu.VMEM((n_tiles, 2 * pitch, TILE), bf16),
            pltpu.VMEM((n_tiles, nodes // 2, TILE), f32),
            pltpu.VMEM((own_tiles, 3, count_k, TILE), f32),
            pltpu.VMEM((3 * nodes, 2 * pitch), bf16),
            pltpu.VMEM((n_tiles, 3, TILE), f32),
            pltpu.VMEM((n_phase, own_tiles, 3, TILE), f32),
            dma((tile_a + 7,)),
            dma((ITERS, 4)),
            dma((ITERS, 4)),
            dma((4,)),
            dma((4,)),
            dma((n_phase,)),
            dma((n_phase,)),
        ],
        compiler_params=pltpu.CompilerParams(
            collective_id=0, has_side_effects=True, vmem_limit_bytes=60 * 1024 * 1024
        ),
    )(
        psi_start[0],
        source[0],
        face_coef,
        diag_coef,
        jnp.transpose(flux_jac, (2, 3, 1, 0)),
        omega,
        metric,
        mode_shape,
        phase_weight,
        pairing[0],
        owner_order[0],
    )
    return (psi_out[None], sens.reshape(count_k, 1, 1, owned))


def solution(mesh):
    sizes = tuple(mesh.shape[name] for name in ("phase", "axial", "radial"))
    return jax.shard_map(
        functools.partial(body, sizes),
        mesh=mesh,
        in_specs=(
            P("phase", None, "axial", "radial", None),
            P("phase", None, "axial", "radial", None),
            P(None, "axial", "radial", None),
            P("axial", "radial", None),
            P(),
            P(),
            P(),
            P(None, None, "axial", "radial", None),
            P("phase"),
            P("axial", "radial", None),
            P("axial", "radial", None),
        ),
        out_specs=(P("phase", None, "axial", "radial", None), P(None, "axial", "radial", "phase")),
        check_vma=False,
    )
```

```python
import functools
import math

import jax
import jax.numpy as jnp
from jax import lax
from jax.experimental import pallas as pl
from jax.experimental.pallas import tpu as pltpu
from jax.sharding import PartitionSpec as P

BLADES = 16
ITERS = 4
RELAX = 0.8
MESH = pl.DeviceIdType.MESH
TILE = 256
TOP = 8


def split(value):
    high = value.astype(jnp.bfloat16)
    return high, (value - high.astype(jnp.float32)).astype(jnp.bfloat16)


def kernel(
    sizes,
    psi_in,
    source_in,
    face_in,
    diag_in,
    flux_in,
    omega_ref,
    metric_ref,
    mode_in,
    weight_ref,
    pairing_in,
    owner_in,
    out_ref,
    sens_ref,
    psi,
    source_ref,
    face_ref,
    diag_ref,
    flux_ref,
    mode_ref,
    pairing_ref,
    owner_ref,
    radial_sent,
    radial_low,
    radial_high,
    face_sent,
    face_low,
    face_high,
    coef,
    inverse,
    wrapped,
    pair_matrix,
    matrix,
    field_high,
    field_low,
    one_hot,
    row_mask,
    sens,
    modes_owned,
    weighted,
    gathered,
    received,
    load_sem,
    send_sem,
    recv_sem,
    face_send_sem,
    face_recv_sem,
    phase_send_sem,
    phase_recv_sem,
):
    n_phase, n_axial, n_radial = sizes
    comps, tile_a, tile_r, pitch = source_ref.shape
    half = comps // 2
    nodes = tile_a * tile_r
    fold = nodes // 2
    n_tiles = owner_ref.shape[1] // TILE
    own_tiles = n_tiles // n_phase
    n_modes = mode_ref.shape[0]
    depth = 6 * comps * TOP
    phase = lax.axis_index("phase")
    ax = lax.axis_index("axial")
    rad = lax.axis_index("radial")
    has_low = (ax > 0, rad > 0)
    has_high = (ax < n_axial - 1, rad < n_radial - 1)
    rows = pl.ds(TOP, tile_r)

    loads = [
        pltpu.make_async_copy(psi_in.at[:, a], psi.at[0, a + 1, :, rows, :], load_sem.at[a])
        for a in range(tile_a)
    ]
    for pair in (
        (face_in, face_ref),
        (flux_in, flux_ref),
        (pairing_in, pairing_ref),
        (diag_in, diag_ref),
        (owner_in, owner_ref),
        (source_in, source_ref),
        (mode_in, mode_ref),
    ):
        loads.append(pltpu.make_async_copy(pair[0], pair[1], load_sem.at[len(loads)]))
    for copy in loads:
        copy.start()

    barrier = pltpu.get_barrier_semaphore()
    for k in range(1, n_phase):
        pl.semaphore_signal(
            barrier,
            inc=1,
            device_id={"phase": lax.rem(phase + k, n_phase)},
            device_id_type=MESH,
        )
    for name, me, low, high in (
        ("axial", ax, has_low[0], has_high[0]),
        ("radial", rad, has_low[1], has_high[1]),
    ):
        @pl.when(low)
        def _():
            pl.semaphore_signal(barrier, inc=1, device_id={name: me - 1}, device_id_type=MESH)

        @pl.when(high)
        def _():
            pl.semaphore_signal(barrier, inc=1, device_id={name: me + 1}, device_id_type=MESH)

    beyond = tile_a + 1 - jnp.where(ax > 0, 0, tile_a + 1)
    coef[jnp.where(ax > 0, 1, 0), beyond] = jnp.zeros((tile_r, pitch), jnp.float32)
    for s in range(ITERS):
        for c in range(comps):
            psi[s, beyond, c, TOP : TOP + tile_r, :] = jnp.zeros((tile_r, pitch), jnp.float32)

    edge = jnp.where(ax > 0, 1, tile_a)
    halo = jnp.where(ax > 0, 0, tile_a + 1)
    first = jnp.where(ax > 0, 2, 1)

    def layer(k):
        return first + k if k < tile_a - 1 else edge

    def half_rows(k):
        return pl.ds(TOP + k * TOP, TOP)

    def axial_copy(s, k, arriving=False):
        return pltpu.make_async_remote_copy(
            src_ref=psi.at[s, edge, :, half_rows(k), :],
            dst_ref=psi.at[s, halo if arriving else tile_a + 1 - halo, :, half_rows(k), :],
            send_sem=send_sem.at[s, k],
            recv_sem=recv_sem.at[s, k],
            device_id={"axial": 1 - ax},
            device_id_type=MESH,
        )

    def radial_copy(s, up, part):
        slots = pl.ds(0, tile_a - 1) if part == 0 else pl.ds(tile_a - 1, 1)
        at = 2 + part * 2 + (0 if up else 1)
        return pltpu.make_async_remote_copy(
            src_ref=radial_sent.at[s, 0 if up else 1, slots],
            dst_ref=(radial_low if up else radial_high).at[s, slots],
            send_sem=send_sem.at[s, at],
            recv_sem=recv_sem.at[s, at],
            device_id={"radial": rad + 1 if up else rad - 1},
            device_id_type=MESH,
        )

    leaving = jnp.where(ax > 0, 1, 0)
    axial_face = 0

    def face_copy(d, arriving=False):
        up = d % 2 == 0
        if d < 2:
            src = coef.at[leaving, edge]
            dst = coef.at[1 - leaving, halo] if arriving else coef.at[leaving, tile_a + 1 - halo]
            target = {"axial": 1 - ax}
        else:
            src = face_sent.at[d - 2]
            dst = face_low if up else face_high
            target = {"radial": rad + 1 if up else rad - 1}
        return pltpu.make_async_remote_copy(
            src_ref=src,
            dst_ref=dst,
            send_sem=face_send_sem.at[d],
            recv_sem=face_recv_sem.at[d],
            device_id=target,
            device_id_type=MESH,
        )

    parts = (range(tile_a - 1), range(tile_a - 1, tile_a))

    def start_radial(s, part):
        for k in parts[part]:
            radial_sent[s, 0, k] = psi[s, layer(k), :, TOP + tile_r - 1, :]
            radial_sent[s, 1, k] = psi[s, layer(k), :, TOP, :]
        for up in (True, False):
            @pl.when((has_high if up else has_low)[1])
            def _():
                radial_copy(s, up, part).start()

    for copy in loads[:tile_a]:
        copy.wait()
    greeted = n_phase - 1 + sum(jnp.where(flag, 1, 0) for flag in has_low + has_high)
    pl.semaphore_wait(barrier, greeted)
    for k in range(2):
        axial_copy(0, k).start()
    for part in range(2):
        start_radial(0, part)

    loads[tile_a].wait()
    for a in range(tile_a):
        for d in range(6):
            coef[d, a + 1] = face_ref[d, a].astype(jnp.float32)
    for a in range(tile_a):
        face_sent[0, a : a + 1, :] = coef[2, a + 1, tile_r - 1 : tile_r, :]
        face_sent[1, a : a + 1, :] = coef[3, a + 1, 0:1, :]
    face_copy(axial_face).start()
    for d in (2, 3):
        @pl.when((has_high if d == 2 else has_low)[1])
        def _():
            face_copy(d).start()

    loads[tile_a + 1].wait()
    real = [flux_ref[j, :, 0, :] for j in range(half)]
    imag = [flux_ref[j, :, 1, :] for j in range(half)]
    fine = lax.Precision.HIGHEST
    entries = (
        jnp.concatenate(real + imag, axis=1),
        jnp.concatenate([-value for value in imag] + real, axis=1),
    )
    tall, wide = comps * TOP, matrix.shape[1]
    spread = jnp.zeros((tall, 6 * comps), jnp.float32)
    row = lax.div(lax.broadcasted_iota(jnp.int32, (tall, half), 0), TOP)
    column = lax.broadcasted_iota(jnp.int32, (tall, half), 1)
    for k in range(2):
        pick = jnp.where(row == column + k * half, 1.0, 0.0)
        spread = spread + jnp.dot(
            pick, entries[k], precision=fine, preferred_element_type=jnp.float32
        )
    row = lax.broadcasted_iota(jnp.int32, (6 * comps, wide), 0)
    column = lax.div(lax.broadcasted_iota(jnp.int32, (6 * comps, wide), 1), TOP)
    spread = jnp.dot(
        spread,
        jnp.where(row == column, 1.0, 0.0),
        precision=fine,
        preferred_element_type=jnp.float32,
    )
    row = lax.rem(lax.broadcasted_iota(jnp.int32, (tall, wide), 0), TOP)
    column = lax.rem(lax.broadcasted_iota(jnp.int32, (tall, wide), 1), TOP)
    high, low = split(jnp.where(row == column, spread, 0.0))
    matrix[:tall] = high
    matrix[tall:] = low
    for slot in range(tile_a):
        for field in (field_high, field_low):
            field[slot, depth:, :] = jnp.zeros((wide - depth, 2 * pitch), jnp.bfloat16)

    loads[tile_a + 2].wait()
    node = lax.broadcasted_iota(jnp.int32, (2 * nodes, nodes), 0)
    partner = jnp.where(node >= nodes, node - nodes, node) == pairing_ref[...]
    pair_matrix[...] = jnp.where(partner, 1.0, 0.0).T.astype(jnp.bfloat16)

    def permuted(value):
        stacked = jnp.concatenate(split(value), axis=0)
        return jnp.dot(pair_matrix[...], stacked, preferred_element_type=jnp.float32)

    lane = lax.broadcasted_iota(jnp.int32, (tile_r, pitch), 1)
    for d, from_lane in ((4, pitch - 1), (5, 0)):
        partner_face = permuted(coef[d, 1 : tile_a + 1].reshape(nodes, pitch))
        for a in range(tile_a):
            own = jnp.where(
                lane == from_lane, partner_face[a * tile_r : (a + 1) * tile_r], coef[d, a + 1]
            )
            coef[d, a + 1] = pltpu.roll(own, 1 if d == 4 else pitch - 1, 1)

    loads[tile_a + 3].wait()
    for a in range(tile_a):
        inverse[a] = RELAX / diag_ref[a]

    angle = 2.0 * math.pi / BLADES
    turn = lax.rem(phase, BLADES)
    cosine = jnp.float32(1.0)
    sine = jnp.float32(0.0)
    for k in range(1, BLADES):
        cosine = jnp.where(turn == k, jnp.float32(math.cos(angle * k)), cosine)
        sine = jnp.where(turn == k, jnp.float32(math.sin(angle * k)), sine)

    def make_one_hot(u, _):
        t = lax.rem(phase * own_tiles + u, n_tiles)
        owner = owner_ref[:, pl.ds(pl.multiple_of(t * TILE, TILE), TILE)]
        row = lax.div(owner, pitch)
        column = owner - row * pitch
        later = row >= fold
        column = jnp.where(later, column + pitch, column)
        row = jnp.where(later, row - fold, row)
        at = lax.broadcasted_iota(jnp.int32, (2 * pitch, TILE), 0)
        one_hot[t] = jnp.where(at == column, 1.0, 0.0).astype(jnp.bfloat16)
        at = lax.broadcasted_iota(jnp.int32, (fold, TILE), 0)
        row_mask[t] = jnp.where(at == row, 1.0, 0.0)
        return 0

    def gather_modes(i, _):
        t = phase * own_tiles + i
        for d in range(3):
            for k in range(0, n_modes, 6):
                part = mode_ref[k : k + 6, d].reshape(6, nodes, pitch)
                left = part[:, :fold].reshape(6 * fold, pitch)
                right = part[:, fold:].reshape(6 * fold, pitch)
                picked = jnp.dot(
                    jnp.concatenate([left, right], axis=1),
                    one_hot[t],
                    preferred_element_type=jnp.float32,
                )
                picked = picked.reshape(6, fold, TILE) * row_mask[t][None]
                modes_owned[i, d, k : k + 6, :] = jnp.sum(picked, axis=1)
        return 0

    low_lane = lane[:TOP]

    def build(s, a, slot, halves):
        for k in halves:
            columns = slice(k * pitch, (k + 1) * pitch)
            here = slice(k * TOP, (k + 1) * TOP)

            def field(layer_at, c, shift):
                at = TOP + k * TOP + shift
                return psi[s, layer_at, c, at : at + TOP, :]

            for c in range(comps):
                own = field(a, c, 0)
                wrap = wrapped[c, a - 1, here]
                scaled = (
                    coef[0, a - 1, here] * field(a - 1, c, 0),
                    coef[1, a + 1, here] * field(a + 1, c, 0),
                    coef[2, a, here] * field(a, c, -1),
                    coef[3, a, here] * field(a, c, 1),
                    coef[4, a, here] * pltpu.roll(jnp.where(low_lane == pitch - 1, wrap, own), 1, 1),
                    coef[5, a, here]
                    * pltpu.roll(jnp.where(low_lane == 0, wrap, own), pitch - 1, 1),
                )
                for d in range(0, 6, 2):
                    at = (c * 6 + d) * TOP
                    high, low = split(jnp.concatenate(scaled[d : d + 2], axis=0))
                    field_high[slot, at : at + 2 * TOP, columns] = high
                    field_low[slot, at : at + 2 * TOP, columns] = low

    def update(s, a, slot, halves):
        columns = slice(halves[0] * pitch, (halves[-1] + 1) * pitch)
        both = jnp.dot(
            matrix[...], field_high[slot, :, columns], preferred_element_type=jnp.float32
        )
        rest = jnp.dot(
            matrix[:tall], field_low[slot, :, columns], preferred_element_type=jnp.float32
        )
        total = both[:tall] + (both[tall:] + rest)
        omega = omega_ref[0]
        for n, k in enumerate(halves):
            here = slice(k * TOP, (k + 1) * TOP)
            there = slice(TOP + k * TOP, 2 * TOP + k * TOP)
            scale = inverse[a - 1, here]

            def incoming(c):
                return total[c * TOP : (c + 1) * TOP, n * pitch : (n + 1) * pitch]

            for i in range(half):
                real = psi[s, a, i, there, :]
                imag = psi[s, a, half + i, there, :]
                got_real = source_ref[i, a - 1, here] - omega * imag + incoming(i)
                got_imag = source_ref[half + i, a - 1, here] + omega * real + incoming(half + i)
                psi[s + 1, a, i, there, :] = (1.0 - RELAX) * real + scale * got_real
                psi[s + 1, a, half + i, there, :] = (1.0 - RELAX) * imag + scale * got_imag

    turned_sine = jnp.where(lane >= pitch // 2, sine, -sine)

    def place_radial(s, part):
        for up in (True, False):
            flag = (has_low if up else has_high)[1]
            at = TOP - 1 if up else TOP + tile_r
            got = radial_low if up else radial_high

            @pl.when(flag)
            def _():
                radial_copy(s, up, part).wait_recv()
                for k in parts[part]:
                    psi[s, layer(k), :, at, :] = got[s, k]

            @pl.when(jnp.logical_not(flag))
            def _():
                for k in parts[part]:
                    psi[s, layer(k), :, at, :] = jnp.zeros((comps, pitch), jnp.float32)

    def section(s, _):
        for c in range(comps):
            whole = psi[s, 1 : tile_a + 1, c, TOP : TOP + tile_r, :].reshape(nodes, pitch)
            wrapped[c] = permuted(whole).reshape(tile_a, tile_r, pitch)
        for a in range(tile_a):
            for j in range(half):
                real, imag = wrapped[j, a], wrapped[half + j, a]
                wrapped[j, a] = cosine * real - turned_sine * imag
                wrapped[half + j, a] = turned_sine * real + cosine * imag

        @pl.when(s == 0)
        def _():
            for copy in loads[tile_a + 4 :]:
                copy.wait()

        place_radial(s, 0)

        @pl.when(s == 0)
        def _():
            for d in (2, 3):
                flag = (has_low if d == 2 else has_high)[1]
                got = face_low if d == 2 else face_high

                @pl.when(flag)
                def _():
                    face_copy(d).wait_recv()

                row = lax.broadcasted_iota(jnp.int32, (tile_r, pitch), 0)
                end = 0 if d == 2 else tile_r - 1
                for a in range(tile_a):
                    moved = pltpu.roll(coef[d, a + 1], 1 if d == 2 else tile_r - 1, 0)
                    coef[d, a + 1] = jnp.where(row == end, 0.0, moved)

                @pl.when(flag)
                def _():
                    for a in range(tile_a):
                        coef[d, a + 1, end : end + 1, :] = got[a : a + 1, :]

        for k in range(tile_a - 1):
            build(s, layer(k), k, (0, 1))
        for k in range(tile_a - 1):
            update(s, layer(k), k, (0, 1))

        @pl.when(s + 1 < ITERS)
        def _():
            start_radial(s + 1, 0)

        lax.fori_loop(
            lax.div(n_tiles * s, ITERS), lax.div(n_tiles * (s + 1), ITERS), make_one_hot, 0
        )
        lax.fori_loop(
            lax.div(own_tiles * s, 2 * ITERS),
            lax.div(own_tiles * (s + 1), 2 * ITERS),
            gather_modes,
            0,
        )
        place_radial(s, 1)

        @pl.when(s == 0)
        def _():
            face_copy(axial_face, arriving=True).wait_recv()

        for k in range(2):
            axial_copy(s, k, arriving=True).wait_recv()
            build(s, edge, tile_a - 1, (k,))
            update(s, edge, tile_a - 1, (k,))

            @pl.when(s + 1 < ITERS)
            def _():
                axial_copy(s + 1, k).start()

        @pl.when(s + 1 < ITERS)
        def _():
            start_radial(s + 1, 1)

        return 0

    lax.fori_loop(0, ITERS, section, 0)

    results = [
        pltpu.make_async_copy(psi.at[ITERS, a + 1, :, rows, :], out_ref.at[:, a], load_sem.at[a])
        for a in range(tile_a)
    ]
    for copy in results:
        copy.start()

    share = weight_ref[0]
    for a in range(tile_a):
        values = [psi[ITERS, a + 1, c, TOP : TOP + tile_r, :] for c in range(comps)]
        row = (a * tile_r) % fold
        column = pitch * ((a * tile_r) // fold)
        for d in range(3):
            height = metric_ref[d, 0] * values[0]
            for c in range(1, comps):
                height = height + metric_ref[d, c] * values[c]
            for part, value in enumerate(split(share * height)):
                at = (part * 3 + d) * fold + row
                weighted[at : at + tile_r, column : column + pitch] = value

    def gather_weighted(t):
        picked = jnp.dot(weighted[...], one_hot[t], preferred_element_type=jnp.float32)
        picked = picked.reshape(2, 3, fold, TILE)
        gathered[t] = jnp.sum((picked[0] + picked[1]) * row_mask[t][None], axis=1)

    def phase_copy(k):
        peer = lax.rem(phase + k, n_phase)
        return pltpu.make_async_remote_copy(
            src_ref=gathered.at[pl.ds(peer * own_tiles, own_tiles)],
            dst_ref=received.at[k],
            send_sem=phase_send_sem.at[k],
            recv_sem=phase_recv_sem.at[k],
            device_id={"phase": peer},
            device_id_type=MESH,
        )

    for k in list(range(1, n_phase)) + [0]:
        peer = lax.rem(phase + k, n_phase)
        for i in range(own_tiles):
            gather_weighted(peer * own_tiles + i)
        if k:
            phase_copy(k).start()

    lax.fori_loop(own_tiles // 2, own_tiles, gather_modes, 0)

    for k in range(1, n_phase):
        phase_copy(k).wait_recv()

    for i in range(own_tiles):
        total = gathered[phase * own_tiles + i]
        for k in range(1, n_phase):
            total = total + received[k, i]
        result = modes_owned[i, 0] * total[0:1]
        for d in range(1, 3):
            result = result + modes_owned[i, d] * total[d : d + 1]
        for k in range(TILE // pitch):
            sens[:, i * (TILE // pitch) + k, :] = result[:, k * pitch : (k + 1) * pitch]

    results.append(pltpu.make_async_copy(sens, sens_ref, load_sem.at[tile_a]))
    results[-1].start()
    for k in range(1, n_phase):
        phase_copy(k).wait_send()
    face_copy(axial_face).wait_send()
    for s in range(ITERS):
        for k in range(2):
            axial_copy(s, k).wait_send()
    for up in (True, False):
        @pl.when((has_high if up else has_low)[1])
        def _():
            face_copy(2 if up else 3).wait_send()
            for s in range(ITERS):
                for part in range(2):
                    radial_copy(s, up, part).wait_send()

    for copy in results:
        copy.wait()


def hand_on(psi_in, sens_in, psi_out, sens_out, sem):
    copies = [pltpu.make_async_copy(sens_in, sens_out, sem.at[0])]
    for c in range(0, psi_in.shape[0], 2):
        own = pl.ds(c, 2)
        copies.append(
            pltpu.make_async_copy(psi_in.at[own], psi_out.at[own], sem.at[1 + c // 2])
        )
    for copy in copies:
        copy.start()
    for copy in copies:
        copy.wait()


def body(
    sizes,
    psi_start,
    source,
    face_coef,
    diag_coef,
    flux_jac,
    omega,
    metric,
    mode_shape,
    phase_weight,
    pairing,
    owner_order,
):
    _, comps, tile_a, tile_r, pitch = psi_start.shape
    half = comps // 2
    nodes = tile_a * tile_r
    cells = nodes * pitch
    n_phase = sizes[0]
    n_tiles = cells // TILE
    own_tiles = n_tiles // n_phase
    owned = cells // n_phase
    count_k = mode_shape.shape[0]
    f32, bf16 = jnp.float32, jnp.bfloat16
    smem = pl.BlockSpec(memory_space=pltpu.SMEM)
    hbm = pl.BlockSpec(memory_space=pltpu.HBM)
    dma = pltpu.SemaphoreType.DMA
    depth = -(-6 * comps * TOP // 128) * 128
    psi_out, sens = pl.pallas_call(
        functools.partial(kernel, sizes),
        out_shape=(
            jax.ShapeDtypeStruct((comps, tile_a, tile_r, pitch), f32),
            jax.ShapeDtypeStruct((count_k, owned // pitch, pitch), f32),
        ),
        in_specs=[hbm, hbm, hbm, hbm, hbm, smem, smem, hbm, smem, hbm, hbm],
        out_specs=(hbm, hbm),
        scratch_shapes=[
            pltpu.VMEM((ITERS + 1, tile_a + 2, comps, tile_r + 2 * TOP, pitch), f32),
            pltpu.VMEM((comps, tile_a, tile_r, pitch), f32),
            pltpu.VMEM((6, tile_a, tile_r, pitch), bf16),
            pltpu.VMEM((tile_a, tile_r, pitch), f32),
            pltpu.VMEM((half, half, 2, 6), f32),
            pltpu.VMEM((count_k, 3, tile_a, tile_r, pitch), bf16),
            pltpu.VMEM((1, nodes), jnp.int32),
            pltpu.VMEM((1, cells), jnp.int32),
            pltpu.VMEM((ITERS, 2, tile_a, comps, pitch), f32),
            pltpu.VMEM((ITERS, tile_a, comps, pitch), f32),
            pltpu.VMEM((ITERS, tile_a, comps, pitch), f32),
            pltpu.VMEM((2, tile_a, pitch), f32),
            pltpu.VMEM((tile_a, pitch), f32),
            pltpu.VMEM((tile_a, pitch), f32),
            pltpu.VMEM((6, tile_a + 2, tile_r, pitch), f32),
            pltpu.VMEM((tile_a, tile_r, pitch), f32),
            pltpu.VMEM((comps, tile_a, tile_r, pitch), f32),
            pltpu.VMEM((nodes, 2 * nodes), bf16),
            pltpu.VMEM((2 * comps * TOP, depth), bf16),
            pltpu.VMEM((tile_a, depth, 2 * pitch), bf16),
            pltpu.VMEM((tile_a, depth, 2 * pitch), bf16),
            pltpu.VMEM((n_tiles, 2 * pitch, TILE), bf16),
            pltpu.VMEM((n_tiles, nodes // 2, TILE), f32),
            pltpu.VMEM((count_k, owned // pitch, pitch), f32),
            pltpu.VMEM((own_tiles, 3, count_k, TILE), f32),
            pltpu.VMEM((3 * nodes, 2 * pitch), bf16),
            pltpu.VMEM((n_tiles, 3, TILE), f32),
            pltpu.VMEM((n_phase, own_tiles, 3, TILE), f32),
            dma((tile_a + 7,)),
            dma((ITERS, 6)),
            dma((ITERS, 6)),
            dma((4,)),
            dma((4,)),
            dma((n_phase,)),
            dma((n_phase,)),
        ],
        compiler_params=pltpu.CompilerParams(
            collective_id=0, has_side_effects=True, vmem_limit_bytes=60 * 1024 * 1024
        ),
    )(
        psi_start[0],
        source[0],
        face_coef,
        diag_coef,
        jnp.transpose(flux_jac, (2, 3, 1, 0)),
        omega,
        metric,
        mode_shape,
        phase_weight,
        pairing[0],
        owner_order[0],
    )
    results = (psi_out, sens)
    psi_out, sens = pl.pallas_call(
        hand_on,
        out_shape=tuple(jax.ShapeDtypeStruct(value.shape, value.dtype) for value in results),
        in_specs=[hbm, hbm],
        out_specs=(hbm, hbm),
        scratch_shapes=[dma((1 + comps // 2,))],
        compiler_params=pltpu.CompilerParams(vmem_limit_bytes=60 * 1024 * 1024),
    )(psi_out, sens)
    return (psi_out[None], sens.reshape(count_k, 1, 1, owned))


def solution(mesh):
    sizes = tuple(mesh.shape[name] for name in ("phase", "axial", "radial"))
    assert sizes[1] == 2
    return jax.shard_map(
        functools.partial(body, sizes),
        mesh=mesh,
        in_specs=(
            P("phase", None, "axial", "radial", None),
            P("phase", None, "axial", "radial", None),
            P(None, "axial", "radial", None),
            P("axial", "radial", None),
            P(),
            P(),
            P(),
            P(None, None, "axial", "radial", None),
            P("phase"),
            P("axial", "radial", None),
            P("axial", "radial", None),
        ),
        out_specs=(P("phase", None, "axial", "radial", None), P(None, "axial", "radial", "phase")),
        check_vma=False,
    )
```

```python
import functools
import math

import jax
import jax.numpy as jnp
from jax import lax
from jax.experimental import pallas as pl
from jax.experimental.pallas import tpu as pltpu
from jax.sharding import PartitionSpec as P

BLADES = 16
ITERS = 4
RELAX = 0.8
MESH = pl.DeviceIdType.MESH
TILE = 256
TOP = 8


def split(value):
    high = value.astype(jnp.bfloat16)
    return high, (value - high.astype(jnp.float32)).astype(jnp.bfloat16)


def kernel(
    sizes,
    psi_in,
    source_in,
    face_in,
    diag_in,
    flux_in,
    omega_ref,
    metric_ref,
    mode_in,
    weight_ref,
    pairing_in,
    owner_in,
    out_ref,
    sens_ref,
    psi,
    source_ref,
    face_ref,
    diag_ref,
    flux_ref,
    mode_ref,
    pairing_ref,
    owner_ref,
    radial_sent,
    radial_low,
    radial_high,
    face_sent,
    face_low,
    face_high,
    coef,
    inverse,
    wrapped,
    pair_matrix,
    matrix,
    field_high,
    field_low,
    one_hot,
    row_mask,
    sens,
    modes_owned,
    weighted,
    gathered,
    received,
    load_sem,
    send_sem,
    recv_sem,
    face_send_sem,
    face_recv_sem,
    phase_send_sem,
    phase_recv_sem,
):
    n_phase, n_axial, n_radial = sizes
    comps, tile_a, tile_r, pitch = source_ref.shape
    half = comps // 2
    nodes = tile_a * tile_r
    fold = nodes // 2
    n_tiles = owner_ref.shape[1] // TILE
    own_tiles = n_tiles // n_phase
    n_modes = mode_ref.shape[0]
    depth = 6 * comps * TOP
    phase = lax.axis_index("phase")
    ax = lax.axis_index("axial")
    rad = lax.axis_index("radial")
    has_low = (ax > 0, rad > 0)
    has_high = (ax < n_axial - 1, rad < n_radial - 1)
    rows = pl.ds(TOP, tile_r)

    loads = [
        pltpu.make_async_copy(psi_in.at[:, a], psi.at[0, a + 1, :, rows, :], load_sem.at[a])
        for a in range(tile_a)
    ]
    for pair in (
        (face_in, face_ref),
        (flux_in, flux_ref),
        (pairing_in, pairing_ref),
        (diag_in, diag_ref),
        (owner_in, owner_ref),
        (source_in, source_ref),
        (mode_in, mode_ref),
    ):
        loads.append(pltpu.make_async_copy(pair[0], pair[1], load_sem.at[len(loads)]))
    for copy in loads:
        copy.start()

    barrier = pltpu.get_barrier_semaphore()
    for k in range(1, n_phase):
        pl.semaphore_signal(
            barrier,
            inc=1,
            device_id={"phase": lax.rem(phase + k, n_phase)},
            device_id_type=MESH,
        )
    for name, me, low, high in (
        ("axial", ax, has_low[0], has_high[0]),
        ("radial", rad, has_low[1], has_high[1]),
    ):
        @pl.when(low)
        def _():
            pl.semaphore_signal(barrier, inc=1, device_id={name: me - 1}, device_id_type=MESH)

        @pl.when(high)
        def _():
            pl.semaphore_signal(barrier, inc=1, device_id={name: me + 1}, device_id_type=MESH)

    beyond = tile_a + 1 - jnp.where(ax > 0, 0, tile_a + 1)
    coef[jnp.where(ax > 0, 1, 0), beyond] = jnp.zeros((tile_r, pitch), jnp.float32)
    for s in range(ITERS):
        for c in range(comps):
            psi[s, beyond, c, TOP : TOP + tile_r, :] = jnp.zeros((tile_r, pitch), jnp.float32)

    edge = jnp.where(ax > 0, 1, tile_a)
    halo = jnp.where(ax > 0, 0, tile_a + 1)
    first = jnp.where(ax > 0, 2, 1)

    def layer(k):
        return first + k if k < tile_a - 1 else edge

    def half_rows(k):
        return pl.ds(TOP + k * TOP, TOP)

    def axial_copy(s, k, arriving=False):
        return pltpu.make_async_remote_copy(
            src_ref=psi.at[s, edge, :, half_rows(k), :],
            dst_ref=psi.at[s, halo if arriving else tile_a + 1 - halo, :, half_rows(k), :],
            send_sem=send_sem.at[s, k],
            recv_sem=recv_sem.at[s, k],
            device_id={"axial": 1 - ax},
            device_id_type=MESH,
        )

    def radial_copy(s, up, part):
        slots = pl.ds(0, tile_a - 1) if part == 0 else pl.ds(tile_a - 1, 1)
        at = 2 + part * 2 + (0 if up else 1)
        return pltpu.make_async_remote_copy(
            src_ref=radial_sent.at[s, 0 if up else 1, slots],
            dst_ref=(radial_low if up else radial_high).at[s, slots],
            send_sem=send_sem.at[s, at],
            recv_sem=recv_sem.at[s, at],
            device_id={"radial": rad + 1 if up else rad - 1},
            device_id_type=MESH,
        )

    leaving = jnp.where(ax > 0, 1, 0)
    axial_face = 0

    def face_copy(d, arriving=False):
        up = d % 2 == 0
        if d < 2:
            src = coef.at[leaving, edge]
            dst = coef.at[1 - leaving, halo] if arriving else coef.at[leaving, tile_a + 1 - halo]
            target = {"axial": 1 - ax}
        else:
            src = face_sent.at[d - 2]
            dst = face_low if up else face_high
            target = {"radial": rad + 1 if up else rad - 1}
        return pltpu.make_async_remote_copy(
            src_ref=src,
            dst_ref=dst,
            send_sem=face_send_sem.at[d],
            recv_sem=face_recv_sem.at[d],
            device_id=target,
            device_id_type=MESH,
        )

    parts = (range(tile_a - 1), range(tile_a - 1, tile_a))

    def start_radial(s, part):
        for k in parts[part]:
            radial_sent[s, 0, k] = psi[s, layer(k), :, TOP + tile_r - 1, :]
            radial_sent[s, 1, k] = psi[s, layer(k), :, TOP, :]
        for up in (True, False):
            @pl.when((has_high if up else has_low)[1])
            def _():
                radial_copy(s, up, part).start()

    loads[tile_a + 1].wait()
    real = [flux_ref[j, :, 0, :] for j in range(half)]
    imag = [flux_ref[j, :, 1, :] for j in range(half)]
    fine = lax.Precision.HIGHEST
    entries = (
        jnp.concatenate(real + imag, axis=1),
        jnp.concatenate([-value for value in imag] + real, axis=1),
    )
    tall, wide = comps * TOP, matrix.shape[1]
    spread = jnp.zeros((tall, 6 * comps), jnp.float32)
    row = lax.div(lax.broadcasted_iota(jnp.int32, (tall, half), 0), TOP)
    column = lax.broadcasted_iota(jnp.int32, (tall, half), 1)
    for k in range(2):
        pick = jnp.where(row == column + k * half, 1.0, 0.0)
        spread = spread + jnp.dot(
            pick, entries[k], precision=fine, preferred_element_type=jnp.float32
        )
    row = lax.broadcasted_iota(jnp.int32, (6 * comps, wide), 0)
    column = lax.div(lax.broadcasted_iota(jnp.int32, (6 * comps, wide), 1), TOP)
    spread = jnp.dot(
        spread,
        jnp.where(row == column, 1.0, 0.0),
        precision=fine,
        preferred_element_type=jnp.float32,
    )
    row = lax.rem(lax.broadcasted_iota(jnp.int32, (tall, wide), 0), TOP)
    column = lax.rem(lax.broadcasted_iota(jnp.int32, (tall, wide), 1), TOP)
    high, low = split(jnp.where(row == column, spread, 0.0))
    matrix[:tall] = high
    matrix[tall:] = low
    for slot in range(tile_a):
        for field in (field_high, field_low):
            field[slot, depth:, :] = jnp.zeros((wide - depth, 2 * pitch), jnp.bfloat16)

    loads[tile_a + 2].wait()
    node = lax.broadcasted_iota(jnp.int32, (2 * nodes, nodes), 0)
    partner = jnp.where(node >= nodes, node - nodes, node) == pairing_ref[...]
    pair_matrix[...] = jnp.where(partner, 1.0, 0.0).T.astype(jnp.bfloat16)

    angle = 2.0 * math.pi / BLADES
    turn = lax.rem(phase, BLADES)
    cosine = jnp.float32(1.0)
    sine = jnp.float32(0.0)
    for k in range(1, BLADES):
        cosine = jnp.where(turn == k, jnp.float32(math.cos(angle * k)), cosine)
        sine = jnp.where(turn == k, jnp.float32(math.sin(angle * k)), sine)

    for copy in loads[:tile_a]:
        copy.wait()
    greeted = n_phase - 1 + sum(jnp.where(flag, 1, 0) for flag in has_low + has_high)
    pl.semaphore_wait(barrier, greeted)
    for k in range(2):
        axial_copy(0, k).start()
    for part in range(2):
        start_radial(0, part)

    loads[tile_a].wait()
    for a in range(tile_a):
        for d in range(6):
            coef[d, a + 1] = face_ref[d, a].astype(jnp.float32)
    for a in range(tile_a):
        face_sent[0, a : a + 1, :] = coef[2, a + 1, tile_r - 1 : tile_r, :]
        face_sent[1, a : a + 1, :] = coef[3, a + 1, 0:1, :]
    face_copy(axial_face).start()
    for d in (2, 3):
        @pl.when((has_high if d == 2 else has_low)[1])
        def _():
            face_copy(d).start()

    def permuted(value):
        stacked = jnp.concatenate(split(value), axis=0)
        return jnp.dot(pair_matrix[...], stacked, preferred_element_type=jnp.float32)

    lane = lax.broadcasted_iota(jnp.int32, (tile_r, pitch), 1)
    for d, from_lane in ((4, pitch - 1), (5, 0)):
        partner_face = permuted(coef[d, 1 : tile_a + 1].reshape(nodes, pitch))
        for a in range(tile_a):
            own = jnp.where(
                lane == from_lane, partner_face[a * tile_r : (a + 1) * tile_r], coef[d, a + 1]
            )
            coef[d, a + 1] = pltpu.roll(own, 1 if d == 4 else pitch - 1, 1)

    loads[tile_a + 3].wait()
    for a in range(tile_a):
        inverse[a] = RELAX / diag_ref[a]

    shift = pitch.bit_length() - 1

    def make_one_hot(v, _):
        for k in range(2):
            t = lax.rem(phase * own_tiles + 2 * v + k, n_tiles)
            owner = owner_ref[:, pl.ds(pl.multiple_of(t * TILE, TILE), TILE)]
            row = owner >> shift
            column = owner & (pitch - 1)
            column = jnp.where(row >= fold, column + pitch, column)
            row = row & (fold - 1)
            at = lax.broadcasted_iota(jnp.int32, (2 * pitch, TILE), 0)
            at, column = at.astype(jnp.bfloat16), column.astype(jnp.bfloat16)
            one, zero = jnp.bfloat16(1.0), jnp.bfloat16(0.0)
            one_hot[t] = jnp.where(at == column, one, zero)
            at = lax.broadcasted_iota(jnp.int32, (fold, TILE), 0)
            row_mask[t] = jnp.where(at == row, 1.0, 0.0)
        return 0

    def gather_modes(i, _):
        t = phase * own_tiles + i
        for d in range(3):
            for k in range(0, n_modes, 6):
                part = mode_ref[k : k + 6, d].reshape(6, nodes, pitch)
                left = part[:, :fold].reshape(6 * fold, pitch)
                right = part[:, fold:].reshape(6 * fold, pitch)
                picked = jnp.dot(
                    jnp.concatenate([left, right], axis=1),
                    one_hot[t],
                    preferred_element_type=jnp.float32,
                )
                picked = picked.reshape(6, fold, TILE) * row_mask[t][None]
                modes_owned[i, d, k : k + 6, :] = jnp.sum(picked, axis=1)
        return 0

    low_lane = lane[:TOP]

    def build(s, a, slot, halves):
        for k in halves:
            columns = slice(k * pitch, (k + 1) * pitch)
            here = slice(k * TOP, (k + 1) * TOP)

            def field(layer_at, c, shift):
                at = TOP + k * TOP + shift
                return psi[s, layer_at, c, at : at + TOP, :]

            for c in range(comps):
                own = field(a, c, 0)
                wrap = wrapped[c, a - 1, here]
                scaled = (
                    coef[0, a - 1, here] * field(a - 1, c, 0),
                    coef[1, a + 1, here] * field(a + 1, c, 0),
                    coef[2, a, here] * field(a, c, -1),
                    coef[3, a, here] * field(a, c, 1),
                    coef[4, a, here] * pltpu.roll(jnp.where(low_lane == pitch - 1, wrap, own), 1, 1),
                    coef[5, a, here]
                    * pltpu.roll(jnp.where(low_lane == 0, wrap, own), pitch - 1, 1),
                )
                for d in range(0, 6, 2):
                    at = (c * 6 + d) * TOP
                    high, low = split(jnp.concatenate(scaled[d : d + 2], axis=0))
                    field_high[slot, at : at + 2 * TOP, columns] = high
                    field_low[slot, at : at + 2 * TOP, columns] = low

    def update(s, a, slot, halves):
        columns = slice(halves[0] * pitch, (halves[-1] + 1) * pitch)
        both = jnp.dot(
            matrix[...], field_high[slot, :, columns], preferred_element_type=jnp.float32
        )
        rest = jnp.dot(
            matrix[:tall], field_low[slot, :, columns], preferred_element_type=jnp.float32
        )
        total = both[:tall] + (both[tall:] + rest)
        omega = omega_ref[0]
        for n, k in enumerate(halves):
            here = slice(k * TOP, (k + 1) * TOP)
            there = slice(TOP + k * TOP, 2 * TOP + k * TOP)
            scale = inverse[a - 1, here]

            def incoming(c):
                return total[c * TOP : (c + 1) * TOP, n * pitch : (n + 1) * pitch]

            for i in range(half):
                real = psi[s, a, i, there, :]
                imag = psi[s, a, half + i, there, :]
                got_real = source_ref[i, a - 1, here] - omega * imag + incoming(i)
                got_imag = source_ref[half + i, a - 1, here] + omega * real + incoming(half + i)
                psi[s + 1, a, i, there, :] = (1.0 - RELAX) * real + scale * got_real
                psi[s + 1, a, half + i, there, :] = (1.0 - RELAX) * imag + scale * got_imag

    turned_sine = jnp.where(lane >= pitch // 2, sine, -sine)

    def place_radial(s, part):
        for up in (True, False):
            flag = (has_low if up else has_high)[1]
            at = TOP - 1 if up else TOP + tile_r
            got = radial_low if up else radial_high

            @pl.when(flag)
            def _():
                radial_copy(s, up, part).wait_recv()
                for k in parts[part]:
                    psi[s, layer(k), :, at, :] = got[s, k]

            @pl.when(jnp.logical_not(flag))
            def _():
                for k in parts[part]:
                    psi[s, layer(k), :, at, :] = jnp.zeros((comps, pitch), jnp.float32)

    def section(s, _):
        for c in range(comps):
            whole = psi[s, 1 : tile_a + 1, c, TOP : TOP + tile_r, :].reshape(nodes, pitch)
            wrapped[c] = permuted(whole).reshape(tile_a, tile_r, pitch)
        for a in range(tile_a):
            for j in range(half):
                real, imag = wrapped[j, a], wrapped[half + j, a]
                wrapped[j, a] = cosine * real - turned_sine * imag
                wrapped[half + j, a] = turned_sine * real + cosine * imag

        @pl.when(s == 0)
        def _():
            for copy in loads[tile_a + 4 :]:
                copy.wait()

        place_radial(s, 0)

        @pl.when(s == 0)
        def _():
            for d in (2, 3):
                flag = (has_low if d == 2 else has_high)[1]
                got = face_low if d == 2 else face_high

                @pl.when(flag)
                def _():
                    face_copy(d).wait_recv()

                row = lax.broadcasted_iota(jnp.int32, (tile_r, pitch), 0)
                end = 0 if d == 2 else tile_r - 1
                for a in range(tile_a):
                    moved = pltpu.roll(coef[d, a + 1], 1 if d == 2 else tile_r - 1, 0)
                    coef[d, a + 1] = jnp.where(row == end, 0.0, moved)

                @pl.when(flag)
                def _():
                    for a in range(tile_a):
                        coef[d, a + 1, end : end + 1, :] = got[a : a + 1, :]

        for k in range(tile_a - 1):
            build(s, layer(k), k, (0, 1))
        for k in range(tile_a - 1):
            update(s, layer(k), k, (0, 1))

        @pl.when(s + 1 < ITERS)
        def _():
            start_radial(s + 1, 0)

        lax.fori_loop(
            lax.div(n_tiles * s, 2 * ITERS), lax.div(n_tiles * (s + 1), 2 * ITERS), make_one_hot, 0
        )
        lax.fori_loop(
            lax.div(own_tiles * s, 2 * ITERS),
            lax.div(own_tiles * (s + 1), 2 * ITERS),
            gather_modes,
            0,
        )
        place_radial(s, 1)

        @pl.when(s == 0)
        def _():
            face_copy(axial_face, arriving=True).wait_recv()

        for k in range(2):
            axial_copy(s, k, arriving=True).wait_recv()
            build(s, edge, tile_a - 1, (k,))
            update(s, edge, tile_a - 1, (k,))

            @pl.when(s + 1 < ITERS)
            def _():
                axial_copy(s + 1, k).start()

        @pl.when(s + 1 < ITERS)
        def _():
            start_radial(s + 1, 1)

        return 0

    lax.fori_loop(0, ITERS, section, 0)

    results = [
        pltpu.make_async_copy(psi.at[ITERS, a + 1, :, rows, :], out_ref.at[:, a], load_sem.at[a])
        for a in range(tile_a)
    ]
    for copy in results:
        copy.start()

    share = weight_ref[0]
    for a in range(tile_a):
        values = [psi[ITERS, a + 1, c, TOP : TOP + tile_r, :] for c in range(comps)]
        row = (a * tile_r) % fold
        column = pitch * ((a * tile_r) // fold)
        for d in range(3):
            height = metric_ref[d, 0] * values[0]
            for c in range(1, comps):
                height = height + metric_ref[d, c] * values[c]
            for part, value in enumerate(split(share * height)):
                at = (part * 3 + d) * fold + row
                weighted[at : at + tile_r, column : column + pitch] = value

    def gather_weighted(t):
        picked = jnp.dot(weighted[...], one_hot[t], preferred_element_type=jnp.float32)
        picked = picked.reshape(2, 3, fold, TILE)
        gathered[t] = jnp.sum((picked[0] + picked[1]) * row_mask[t][None], axis=1)

    def phase_copy(k):
        peer = lax.rem(phase + k, n_phase)
        return pltpu.make_async_remote_copy(
            src_ref=gathered.at[pl.ds(peer * own_tiles, own_tiles)],
            dst_ref=received.at[k],
            send_sem=phase_send_sem.at[k],
            recv_sem=phase_recv_sem.at[k],
            device_id={"phase": peer},
            device_id_type=MESH,
        )

    for k in list(range(1, n_phase)) + [0]:
        peer = lax.rem(phase + k, n_phase)
        for i in range(own_tiles):
            gather_weighted(peer * own_tiles + i)
        if k:
            phase_copy(k).start()

    lax.fori_loop(own_tiles // 2, own_tiles, gather_modes, 0)

    for k in range(1, n_phase):
        phase_copy(k).wait_recv()

    for i in range(own_tiles):
        total = gathered[phase * own_tiles + i]
        for k in range(1, n_phase):
            total = total + received[k, i]
        result = modes_owned[i, 0] * total[0:1]
        for d in range(1, 3):
            result = result + modes_owned[i, d] * total[d : d + 1]
        for k in range(TILE // pitch):
            sens[:, i * (TILE // pitch) + k, :] = result[:, k * pitch : (k + 1) * pitch]

    results.append(pltpu.make_async_copy(sens, sens_ref, load_sem.at[tile_a]))
    results[-1].start()
    for k in range(1, n_phase):
        phase_copy(k).wait_send()
    face_copy(axial_face).wait_send()
    for s in range(ITERS):
        for k in range(2):
            axial_copy(s, k).wait_send()
    for up in (True, False):
        @pl.when((has_high if up else has_low)[1])
        def _():
            face_copy(2 if up else 3).wait_send()
            for s in range(ITERS):
                for part in range(2):
                    radial_copy(s, up, part).wait_send()

    for copy in results:
        copy.wait()


def hand_on(psi_in, sens_in, psi_out, sens_out, psi, sens, sem):
    steps = [(sens_in, sens, sens_out)]
    for c in range(0, psi_in.shape[0], 2):
        own = pl.ds(c, 2)
        steps.append((psi_in.at[own], psi.at[own], psi_out.at[own]))
    arrive = [pltpu.make_async_copy(p, q, sem.at[0, k]) for k, (p, q, _) in enumerate(steps)]
    leave = [pltpu.make_async_copy(q, r, sem.at[1, k]) for k, (_, q, r) in enumerate(steps)]
    for copy in arrive:
        copy.start()
    for k in range(len(steps)):
        arrive[k].wait()
        leave[k].start()
    for copy in leave:
        copy.wait()


def body(
    sizes,
    psi_start,
    source,
    face_coef,
    diag_coef,
    flux_jac,
    omega,
    metric,
    mode_shape,
    phase_weight,
    pairing,
    owner_order,
):
    _, comps, tile_a, tile_r, pitch = psi_start.shape
    half = comps // 2
    nodes = tile_a * tile_r
    cells = nodes * pitch
    n_phase = sizes[0]
    n_tiles = cells // TILE
    own_tiles = n_tiles // n_phase
    owned = cells // n_phase
    count_k = mode_shape.shape[0]
    f32, bf16 = jnp.float32, jnp.bfloat16
    smem = pl.BlockSpec(memory_space=pltpu.SMEM)
    hbm = pl.BlockSpec(memory_space=pltpu.HBM)
    dma = pltpu.SemaphoreType.DMA
    depth = -(-6 * comps * TOP // 128) * 128
    psi_out, sens = pl.pallas_call(
        functools.partial(kernel, sizes),
        out_shape=(
            jax.ShapeDtypeStruct((comps, tile_a, tile_r, pitch), f32),
            jax.ShapeDtypeStruct((count_k, owned // pitch, pitch), f32),
        ),
        in_specs=[hbm, hbm, hbm, hbm, hbm, smem, smem, hbm, smem, hbm, hbm],
        out_specs=(hbm, hbm),
        scratch_shapes=[
            pltpu.VMEM((ITERS + 1, tile_a + 2, comps, tile_r + 2 * TOP, pitch), f32),
            pltpu.VMEM((comps, tile_a, tile_r, pitch), f32),
            pltpu.VMEM((6, tile_a, tile_r, pitch), bf16),
            pltpu.VMEM((tile_a, tile_r, pitch), f32),
            pltpu.VMEM((half, half, 2, 6), f32),
            pltpu.VMEM((count_k, 3, tile_a, tile_r, pitch), bf16),
            pltpu.VMEM((1, nodes), jnp.int32),
            pltpu.VMEM((1, cells), jnp.int32),
            pltpu.VMEM((ITERS, 2, tile_a, comps, pitch), f32),
            pltpu.VMEM((ITERS, tile_a, comps, pitch), f32),
            pltpu.VMEM((ITERS, tile_a, comps, pitch), f32),
            pltpu.VMEM((2, tile_a, pitch), f32),
            pltpu.VMEM((tile_a, pitch), f32),
            pltpu.VMEM((tile_a, pitch), f32),
            pltpu.VMEM((6, tile_a + 2, tile_r, pitch), f32),
            pltpu.VMEM((tile_a, tile_r, pitch), f32),
            pltpu.VMEM((comps, tile_a, tile_r, pitch), f32),
            pltpu.VMEM((nodes, 2 * nodes), bf16),
            pltpu.VMEM((2 * comps * TOP, depth), bf16),
            pltpu.VMEM((tile_a, depth, 2 * pitch), bf16),
            pltpu.VMEM((tile_a, depth, 2 * pitch), bf16),
            pltpu.VMEM((n_tiles, 2 * pitch, TILE), bf16),
            pltpu.VMEM((n_tiles, nodes // 2, TILE), f32),
            pltpu.VMEM((count_k, owned // pitch, pitch), f32),
            pltpu.VMEM((own_tiles, 3, count_k, TILE), f32),
            pltpu.VMEM((3 * nodes, 2 * pitch), bf16),
            pltpu.VMEM((n_tiles, 3, TILE), f32),
            pltpu.VMEM((n_phase, own_tiles, 3, TILE), f32),
            dma((tile_a + 7,)),
            dma((ITERS, 6)),
            dma((ITERS, 6)),
            dma((4,)),
            dma((4,)),
            dma((n_phase,)),
            dma((n_phase,)),
        ],
        compiler_params=pltpu.CompilerParams(
            collective_id=0, has_side_effects=True, vmem_limit_bytes=60 * 1024 * 1024
        ),
    )(
        psi_start[0],
        source[0],
        face_coef,
        diag_coef,
        jnp.transpose(flux_jac, (2, 3, 1, 0)),
        omega,
        metric,
        mode_shape,
        phase_weight,
        pairing[0],
        owner_order[0],
    )
    results = (psi_out, sens)
    psi_out, sens = pl.pallas_call(
        hand_on,
        out_shape=tuple(jax.ShapeDtypeStruct(value.shape, value.dtype) for value in results),
        in_specs=[hbm, hbm],
        out_specs=(hbm, hbm),
        scratch_shapes=[pltpu.VMEM(value.shape, value.dtype) for value in results]
        + [dma((2, 1 + comps // 2))],
        compiler_params=pltpu.CompilerParams(vmem_limit_bytes=60 * 1024 * 1024),
    )(psi_out, sens)
    return (psi_out[None], sens.reshape(count_k, 1, 1, owned))


def solution(mesh):
    sizes = tuple(mesh.shape[name] for name in ("phase", "axial", "radial"))
    assert sizes[1] == 2
    return jax.shard_map(
        functools.partial(body, sizes),
        mesh=mesh,
        in_specs=(
            P("phase", None, "axial", "radial", None),
            P("phase", None, "axial", "radial", None),
            P(None, "axial", "radial", None),
            P("axial", "radial", None),
            P(),
            P(),
            P(),
            P(None, None, "axial", "radial", None),
            P("phase"),
            P("axial", "radial", None),
            P("axial", "radial", None),
        ),
        out_specs=(P("phase", None, "axial", "radial", None), P(None, "axial", "radial", "phase")),
        check_vma=False,
    )
```

```python
import functools
import math

import jax
import jax.numpy as jnp
from jax import lax
from jax.experimental import pallas as pl
from jax.experimental.pallas import tpu as pltpu
from jax.sharding import PartitionSpec as P

BLADES = 16
ITERS = 4
RELAX = 0.8
MESH = pl.DeviceIdType.MESH
TILE = 256
TOP = 8


def split(value):
    high = value.astype(jnp.bfloat16)
    return high, (value - high.astype(jnp.float32)).astype(jnp.bfloat16)


def kernel(
    sizes,
    psi_in,
    source_in,
    face_in,
    diag_in,
    flux_in,
    omega_ref,
    metric_ref,
    mode_in,
    weight_ref,
    pairing_in,
    owner_in,
    out_ref,
    sens_ref,
    psi,
    source_ref,
    face_ref,
    diag_ref,
    flux_ref,
    mode_ref,
    pairing_ref,
    owner_ref,
    radial_sent,
    radial_low,
    radial_high,
    face_sent,
    face_low,
    face_high,
    coef,
    inverse,
    wrapped,
    pair_matrix,
    matrix,
    field_high,
    field_low,
    one_hot,
    row_mask,
    sens,
    modes_owned,
    weighted,
    gathered,
    received,
    load_sem,
    send_sem,
    recv_sem,
    face_send_sem,
    face_recv_sem,
    phase_send_sem,
    phase_recv_sem,
):
    n_phase, n_axial, n_radial = sizes
    comps, tile_a, tile_r, pitch = source_ref.shape
    half = comps // 2
    nodes = tile_a * tile_r
    fold = nodes // 2
    n_tiles = owner_ref.shape[1] // TILE
    own_tiles = n_tiles // n_phase
    n_modes = mode_ref.shape[0]
    depth = 6 * comps * TOP
    phase = lax.axis_index("phase")
    ax = lax.axis_index("axial")
    rad = lax.axis_index("radial")
    has_low = (ax > 0, rad > 0)
    has_high = (ax < n_axial - 1, rad < n_radial - 1)
    rows = pl.ds(TOP, tile_r)

    loads = [
        pltpu.make_async_copy(psi_in.at[:, a], psi.at[0, a + 1, :, rows, :], load_sem.at[a])
        for a in range(tile_a)
    ]
    for pair in (
        (face_in, face_ref),
        (flux_in, flux_ref),
        (pairing_in, pairing_ref),
        (diag_in, diag_ref),
        (owner_in, owner_ref),
        (source_in, source_ref),
        (mode_in, mode_ref),
    ):
        loads.append(pltpu.make_async_copy(pair[0], pair[1], load_sem.at[len(loads)]))
    for copy in loads:
        copy.start()

    barrier = pltpu.get_barrier_semaphore()
    for k in range(1, n_phase):
        pl.semaphore_signal(
            barrier,
            inc=1,
            device_id={"phase": lax.rem(phase + k, n_phase)},
            device_id_type=MESH,
        )
    for name, me, low, high in (
        ("axial", ax, has_low[0], has_high[0]),
        ("radial", rad, has_low[1], has_high[1]),
    ):
        @pl.when(low)
        def _():
            pl.semaphore_signal(barrier, inc=1, device_id={name: me - 1}, device_id_type=MESH)

        @pl.when(high)
        def _():
            pl.semaphore_signal(barrier, inc=1, device_id={name: me + 1}, device_id_type=MESH)

    beyond = tile_a + 1 - jnp.where(ax > 0, 0, tile_a + 1)
    coef[jnp.where(ax > 0, 1, 0), beyond] = jnp.zeros((tile_r, pitch), jnp.float32)
    for s in range(ITERS):
        for c in range(comps):
            psi[s, beyond, c, TOP : TOP + tile_r, :] = jnp.zeros((tile_r, pitch), jnp.float32)

    edge = jnp.where(ax > 0, 1, tile_a)
    halo = jnp.where(ax > 0, 0, tile_a + 1)
    first = jnp.where(ax > 0, 2, 1)

    def layer(k):
        return first + k if k < tile_a - 1 else edge

    def half_rows(k):
        return pl.ds(TOP + k * TOP, TOP)

    def axial_copy(s, k, arriving=False, source=None):
        return pltpu.make_async_remote_copy(
            src_ref=psi.at[s, edge, :, half_rows(k), :] if source is None else source,
            dst_ref=psi.at[s, halo if arriving else tile_a + 1 - halo, :, half_rows(k), :],
            send_sem=send_sem.at[s, k],
            recv_sem=recv_sem.at[s, k],
            device_id={"axial": 1 - ax},
            device_id_type=MESH,
        )

    def radial_copy(s, up, part):
        slots = pl.ds(0, tile_a - 1) if part == 0 else pl.ds(tile_a - 1, 1)
        at = 2 + part * 2 + (0 if up else 1)
        return pltpu.make_async_remote_copy(
            src_ref=radial_sent.at[s, 0 if up else 1, slots],
            dst_ref=(radial_low if up else radial_high).at[s, slots],
            send_sem=send_sem.at[s, at],
            recv_sem=recv_sem.at[s, at],
            device_id={"radial": rad + 1 if up else rad - 1},
            device_id_type=MESH,
        )

    leaving = jnp.where(ax > 0, 1, 0)
    axial_face = 0

    def face_copy(d, arriving=False):
        up = d % 2 == 0
        if d < 2:
            src = coef.at[leaving, edge]
            dst = coef.at[1 - leaving, halo] if arriving else coef.at[leaving, tile_a + 1 - halo]
            target = {"axial": 1 - ax}
        else:
            src = face_sent.at[d - 2]
            dst = face_low if up else face_high
            target = {"radial": rad + 1 if up else rad - 1}
        return pltpu.make_async_remote_copy(
            src_ref=src,
            dst_ref=dst,
            send_sem=face_send_sem.at[d],
            recv_sem=face_recv_sem.at[d],
            device_id=target,
            device_id_type=MESH,
        )

    parts = (range(tile_a - 1), range(tile_a - 1, tile_a))

    def start_radial(s, part):
        for k in parts[part]:
            radial_sent[s, 0, k] = psi[s, layer(k), :, TOP + tile_r - 1, :]
            radial_sent[s, 1, k] = psi[s, layer(k), :, TOP, :]
        for up in (True, False):
            @pl.when((has_high if up else has_low)[1])
            def _():
                radial_copy(s, up, part).start()

    greeted = n_phase - 1 + sum(jnp.where(flag, 1, 0) for flag in has_low + has_high)
    pl.semaphore_wait(barrier, greeted)
    for k in range(2):
        axial_copy(0, k, source=psi_in.at[:, edge - 1, pl.ds(k * TOP, TOP), :]).start()
    for copy in loads[:tile_a]:
        copy.wait()
    for part in range(2):
        start_radial(0, part)

    loads[tile_a].wait()
    for a in range(tile_a):
        for d in range(6):
            coef[d, a + 1] = face_ref[d, a].astype(jnp.float32)
    for a in range(tile_a):
        face_sent[0, a : a + 1, :] = coef[2, a + 1, tile_r - 1 : tile_r, :]
        face_sent[1, a : a + 1, :] = coef[3, a + 1, 0:1, :]
    face_copy(axial_face).start()
    for d in (2, 3):
        @pl.when((has_high if d == 2 else has_low)[1])
        def _():
            face_copy(d).start()

    loads[tile_a + 1].wait()
    real = [flux_ref[j, :, 0, :] for j in range(half)]
    imag = [flux_ref[j, :, 1, :] for j in range(half)]
    fine = lax.Precision.HIGHEST
    entries = (
        jnp.concatenate(real + imag, axis=1),
        jnp.concatenate([-value for value in imag] + real, axis=1),
    )
    tall, wide = comps * TOP, matrix.shape[1]
    spread = jnp.zeros((tall, 6 * comps), jnp.float32)
    row = lax.div(lax.broadcasted_iota(jnp.int32, (tall, half), 0), TOP)
    column = lax.broadcasted_iota(jnp.int32, (tall, half), 1)
    for k in range(2):
        pick = jnp.where(row == column + k * half, 1.0, 0.0)
        spread = spread + jnp.dot(
            pick, entries[k], precision=fine, preferred_element_type=jnp.float32
        )
    row = lax.broadcasted_iota(jnp.int32, (6 * comps, wide), 0)
    column = lax.div(lax.broadcasted_iota(jnp.int32, (6 * comps, wide), 1), TOP)
    spread = jnp.dot(
        spread,
        jnp.where(row == column, 1.0, 0.0),
        precision=fine,
        preferred_element_type=jnp.float32,
    )
    row = lax.rem(lax.broadcasted_iota(jnp.int32, (tall, wide), 0), TOP)
    column = lax.rem(lax.broadcasted_iota(jnp.int32, (tall, wide), 1), TOP)
    high, low = split(jnp.where(row == column, spread, 0.0))
    matrix[:tall] = high
    matrix[tall:] = low
    for slot in range(tile_a):
        for field in (field_high, field_low):
            field[slot, depth:, :] = jnp.zeros((wide - depth, 2 * pitch), jnp.bfloat16)

    loads[tile_a + 2].wait()
    node = lax.broadcasted_iota(jnp.int32, (2 * nodes, nodes), 0)
    partner = jnp.where(node >= nodes, node - nodes, node) == pairing_ref[...]
    pair_matrix[...] = jnp.where(partner, 1.0, 0.0).T.astype(jnp.bfloat16)

    angle = 2.0 * math.pi / BLADES
    turn = lax.rem(phase, BLADES)
    cosine = jnp.float32(1.0)
    sine = jnp.float32(0.0)
    for k in range(1, BLADES):
        cosine = jnp.where(turn == k, jnp.float32(math.cos(angle * k)), cosine)
        sine = jnp.where(turn == k, jnp.float32(math.sin(angle * k)), sine)

    def permuted(value):
        stacked = jnp.concatenate(split(value), axis=0)
        return jnp.dot(pair_matrix[...], stacked, preferred_element_type=jnp.float32)

    lane = lax.broadcasted_iota(jnp.int32, (tile_r, pitch), 1)
    for d, from_lane in ((4, pitch - 1), (5, 0)):
        partner_face = permuted(coef[d, 1 : tile_a + 1].reshape(nodes, pitch))
        for a in range(tile_a):
            own = jnp.where(
                lane == from_lane, partner_face[a * tile_r : (a + 1) * tile_r], coef[d, a + 1]
            )
            coef[d, a + 1] = pltpu.roll(own, 1 if d == 4 else pitch - 1, 1)

    loads[tile_a + 3].wait()
    for a in range(tile_a):
        inverse[a] = RELAX / diag_ref[a]

    shift = pitch.bit_length() - 1

    def make_one_hot(v, _):
        for k in range(2):
            t = lax.rem(phase * own_tiles + 2 * v + k, n_tiles)
            owner = owner_ref[:, pl.ds(pl.multiple_of(t * TILE, TILE), TILE)]
            row = owner >> shift
            column = owner & (pitch - 1)
            column = jnp.where(row >= fold, column + pitch, column)
            row = row & (fold - 1)
            at = lax.broadcasted_iota(jnp.int32, (2 * pitch, TILE), 0)
            at, column = at.astype(jnp.bfloat16), column.astype(jnp.bfloat16)
            one, zero = jnp.bfloat16(1.0), jnp.bfloat16(0.0)
            one_hot[t] = jnp.where(at == column, one, zero)
            at = lax.broadcasted_iota(jnp.int32, (fold, TILE), 0)
            row_mask[t] = jnp.where(at == row, 1.0, 0.0)
        return 0

    def gather_modes(i, _):
        t = phase * own_tiles + i
        for d in range(3):
            for k in range(0, n_modes, 6):
                part = mode_ref[k : k + 6, d].reshape(6, nodes, pitch)
                left = part[:, :fold].reshape(6 * fold, pitch)
                right = part[:, fold:].reshape(6 * fold, pitch)
                picked = jnp.dot(
                    jnp.concatenate([left, right], axis=1),
                    one_hot[t],
                    preferred_element_type=jnp.float32,
                )
                picked = picked.reshape(6, fold, TILE) * row_mask[t][None]
                modes_owned[i, d, k : k + 6, :] = jnp.sum(picked, axis=1)
        return 0

    low_lane = lane[:TOP]

    def build(s, a, slot, halves):
        for k in halves:
            columns = slice(k * pitch, (k + 1) * pitch)
            here = slice(k * TOP, (k + 1) * TOP)

            def field(layer_at, c, shift):
                at = TOP + k * TOP + shift
                return psi[s, layer_at, c, at : at + TOP, :]

            for c in range(comps):
                own = field(a, c, 0)
                wrap = wrapped[c, a - 1, here]
                scaled = (
                    coef[0, a - 1, here] * field(a - 1, c, 0),
                    coef[1, a + 1, here] * field(a + 1, c, 0),
                    coef[2, a, here] * field(a, c, -1),
                    coef[3, a, here] * field(a, c, 1),
                    coef[4, a, here] * pltpu.roll(jnp.where(low_lane == pitch - 1, wrap, own), 1, 1),
                    coef[5, a, here]
                    * pltpu.roll(jnp.where(low_lane == 0, wrap, own), pitch - 1, 1),
                )
                for d in range(0, 6, 2):
                    at = (c * 6 + d) * TOP
                    high, low = split(jnp.concatenate(scaled[d : d + 2], axis=0))
                    field_high[slot, at : at + 2 * TOP, columns] = high
                    field_low[slot, at : at + 2 * TOP, columns] = low

    def update(s, a, slot, halves):
        columns = slice(halves[0] * pitch, (halves[-1] + 1) * pitch)
        both = jnp.dot(
            matrix[...], field_high[slot, :, columns], preferred_element_type=jnp.float32
        )
        rest = jnp.dot(
            matrix[:tall], field_low[slot, :, columns], preferred_element_type=jnp.float32
        )
        total = both[:tall] + (both[tall:] + rest)
        omega = omega_ref[0]
        for n, k in enumerate(halves):
            here = slice(k * TOP, (k + 1) * TOP)
            there = slice(TOP + k * TOP, 2 * TOP + k * TOP)
            scale = inverse[a - 1, here]

            def incoming(c):
                return total[c * TOP : (c + 1) * TOP, n * pitch : (n + 1) * pitch]

            for i in range(half):
                real = psi[s, a, i, there, :]
                imag = psi[s, a, half + i, there, :]
                got_real = source_ref[i, a - 1, here] - omega * imag + incoming(i)
                got_imag = source_ref[half + i, a - 1, here] + omega * real + incoming(half + i)
                psi[s + 1, a, i, there, :] = (1.0 - RELAX) * real + scale * got_real
                psi[s + 1, a, half + i, there, :] = (1.0 - RELAX) * imag + scale * got_imag

    face_lane = lax.broadcasted_iota(jnp.int32, (nodes, pitch), 1)
    turned_sine = jnp.where(face_lane >= pitch // 2, sine, -sine)

    def place_radial(s, part):
        for up in (True, False):
            flag = (has_low if up else has_high)[1]
            at = TOP - 1 if up else TOP + tile_r
            got = radial_low if up else radial_high

            @pl.when(flag)
            def _():
                radial_copy(s, up, part).wait_recv()
                for k in parts[part]:
                    psi[s, layer(k), :, at, :] = got[s, k]

            @pl.when(jnp.logical_not(flag))
            def _():
                for k in parts[part]:
                    psi[s, layer(k), :, at, :] = jnp.zeros((comps, pitch), jnp.float32)

    def section(s, _):
        for j in range(half):
            pair = [
                psi[s, 1 : tile_a + 1, c, TOP : TOP + tile_r, :].reshape(nodes, pitch)
                for c in (j, half + j)
            ]
            both = permuted(jnp.concatenate(pair, axis=1))
            real, imag = both[:, :pitch], both[:, pitch:]
            turned = (cosine * real - turned_sine * imag, turned_sine * real + cosine * imag)
            for c, value in zip((j, half + j), turned):
                wrapped[c] = value.reshape(tile_a, tile_r, pitch)

        @pl.when(s == 0)
        def _():
            for copy in loads[tile_a + 4 :]:
                copy.wait()

        place_radial(s, 0)

        @pl.when(s == 0)
        def _():
            for d in (2, 3):
                flag = (has_low if d == 2 else has_high)[1]
                got = face_low if d == 2 else face_high

                @pl.when(flag)
                def _():
                    face_copy(d).wait_recv()

                row = lax.broadcasted_iota(jnp.int32, (tile_r, pitch), 0)
                end = 0 if d == 2 else tile_r - 1
                for a in range(tile_a):
                    moved = pltpu.roll(coef[d, a + 1], 1 if d == 2 else tile_r - 1, 0)
                    coef[d, a + 1] = jnp.where(row == end, 0.0, moved)

                @pl.when(flag)
                def _():
                    for a in range(tile_a):
                        coef[d, a + 1, end : end + 1, :] = got[a : a + 1, :]

        for k in range(tile_a - 1):
            build(s, layer(k), k, (0, 1))
        for k in range(tile_a - 1):
            update(s, layer(k), k, (0, 1))

        @pl.when(s + 1 < ITERS)
        def _():
            start_radial(s + 1, 0)

        lax.fori_loop(
            lax.div(n_tiles * s, 2 * ITERS), lax.div(n_tiles * (s + 1), 2 * ITERS), make_one_hot, 0
        )
        lax.fori_loop(
            lax.div(own_tiles * s, 2 * ITERS),
            lax.div(own_tiles * (s + 1), 2 * ITERS),
            gather_modes,
            0,
        )
        place_radial(s, 1)

        @pl.when(s == 0)
        def _():
            face_copy(axial_face, arriving=True).wait_recv()

        for k in range(2):
            axial_copy(s, k, arriving=True).wait_recv()
            build(s, edge, tile_a - 1, (k,))
            update(s, edge, tile_a - 1, (k,))

            @pl.when(s + 1 < ITERS)
            def _():
                axial_copy(s + 1, k).start()

        @pl.when(s + 1 < ITERS)
        def _():
            start_radial(s + 1, 1)

        return 0

    lax.fori_loop(0, ITERS, section, 0)

    results = [
        pltpu.make_async_copy(psi.at[ITERS, a + 1, :, rows, :], out_ref.at[:, a], load_sem.at[a])
        for a in range(tile_a)
    ]
    for copy in results:
        copy.start()

    share = weight_ref[0]
    for a in range(tile_a):
        values = [psi[ITERS, a + 1, c, TOP : TOP + tile_r, :] for c in range(comps)]
        row = (a * tile_r) % fold
        column = pitch * ((a * tile_r) // fold)
        for d in range(3):
            height = metric_ref[d, 0] * values[0]
            for c in range(1, comps):
                height = height + metric_ref[d, c] * values[c]
            for part, value in enumerate(split(share * height)):
                at = (part * 3 + d) * fold + row
                weighted[at : at + tile_r, column : column + pitch] = value

    def gather_weighted(t):
        picked = jnp.dot(weighted[...], one_hot[t], preferred_element_type=jnp.float32)
        picked = picked.reshape(2, 3, fold, TILE)
        gathered[t] = jnp.sum((picked[0] + picked[1]) * row_mask[t][None], axis=1)

    def phase_copy(k):
        peer = lax.rem(phase + k, n_phase)
        return pltpu.make_async_remote_copy(
            src_ref=gathered.at[pl.ds(peer * own_tiles, own_tiles)],
            dst_ref=received.at[k],
            send_sem=phase_send_sem.at[k],
            recv_sem=phase_recv_sem.at[k],
            device_id={"phase": peer},
            device_id_type=MESH,
        )

    for k in list(range(1, n_phase)) + [0]:
        peer = lax.rem(phase + k, n_phase)
        for i in range(own_tiles):
            gather_weighted(peer * own_tiles + i)
        if k:
            phase_copy(k).start()

    lax.fori_loop(own_tiles // 2, own_tiles, gather_modes, 0)

    for k in range(1, n_phase):
        phase_copy(k).wait_recv()

    for i in range(own_tiles):
        total = gathered[phase * own_tiles + i]
        for k in range(1, n_phase):
            total = total + received[k, i]
        result = modes_owned[i, 0] * total[0:1]
        for d in range(1, 3):
            result = result + modes_owned[i, d] * total[d : d + 1]
        for k in range(TILE // pitch):
            sens[:, i * (TILE // pitch) + k, :] = result[:, k * pitch : (k + 1) * pitch]

    results.append(pltpu.make_async_copy(sens, sens_ref, load_sem.at[tile_a]))
    results[-1].start()
    for k in range(1, n_phase):
        phase_copy(k).wait_send()
    face_copy(axial_face).wait_send()
    for s in range(ITERS):
        for k in range(2):
            from_input = psi_in.at[:, edge - 1, pl.ds(k * TOP, TOP), :] if s == 0 else None
            axial_copy(s, k, source=from_input).wait_send()
    for up in (True, False):
        @pl.when((has_high if up else has_low)[1])
        def _():
            face_copy(2 if up else 3).wait_send()
            for s in range(ITERS):
                for part in range(2):
                    radial_copy(s, up, part).wait_send()

    for copy in results:
        copy.wait()


def hand_on(psi_in, sens_in, psi_out, sens_out, psi, sens, sem):
    steps = [(sens_in, sens, sens_out)]
    for c in range(0, psi_in.shape[0], 2):
        own = pl.ds(c, 2)
        steps.append((psi_in.at[own], psi.at[own], psi_out.at[own]))
    arrive = [pltpu.make_async_copy(p, q, sem.at[0, k]) for k, (p, q, _) in enumerate(steps)]
    leave = [pltpu.make_async_copy(q, r, sem.at[1, k]) for k, (_, q, r) in enumerate(steps)]
    for copy in arrive:
        copy.start()
    for k in range(len(steps)):
        arrive[k].wait()
        leave[k].start()
    for copy in leave:
        copy.wait()


def body(
    sizes,
    psi_start,
    source,
    face_coef,
    diag_coef,
    flux_jac,
    omega,
    metric,
    mode_shape,
    phase_weight,
    pairing,
    owner_order,
):
    _, comps, tile_a, tile_r, pitch = psi_start.shape
    half = comps // 2
    nodes = tile_a * tile_r
    cells = nodes * pitch
    n_phase = sizes[0]
    n_tiles = cells // TILE
    own_tiles = n_tiles // n_phase
    owned = cells // n_phase
    count_k = mode_shape.shape[0]
    f32, bf16 = jnp.float32, jnp.bfloat16
    smem = pl.BlockSpec(memory_space=pltpu.SMEM)
    hbm = pl.BlockSpec(memory_space=pltpu.HBM)
    dma = pltpu.SemaphoreType.DMA
    depth = -(-6 * comps * TOP // 128) * 128
    psi_out, sens = pl.pallas_call(
        functools.partial(kernel, sizes),
        out_shape=(
            jax.ShapeDtypeStruct((comps, tile_a, tile_r, pitch), f32),
            jax.ShapeDtypeStruct((count_k, owned // pitch, pitch), f32),
        ),
        in_specs=[hbm, hbm, hbm, hbm, hbm, smem, smem, hbm, smem, hbm, hbm],
        out_specs=(hbm, hbm),
        scratch_shapes=[
            pltpu.VMEM((ITERS + 1, tile_a + 2, comps, tile_r + 2 * TOP, pitch), f32),
            pltpu.VMEM((comps, tile_a, tile_r, pitch), f32),
            pltpu.VMEM((6, tile_a, tile_r, pitch), bf16),
            pltpu.VMEM((tile_a, tile_r, pitch), f32),
            pltpu.VMEM((half, half, 2, 6), f32),
            pltpu.VMEM((count_k, 3, tile_a, tile_r, pitch), bf16),
            pltpu.VMEM((1, nodes), jnp.int32),
            pltpu.VMEM((1, cells), jnp.int32),
            pltpu.VMEM((ITERS, 2, tile_a, comps, pitch), f32),
            pltpu.VMEM((ITERS, tile_a, comps, pitch), f32),
            pltpu.VMEM((ITERS, tile_a, comps, pitch), f32),
            pltpu.VMEM((2, tile_a, pitch), f32),
            pltpu.VMEM((tile_a, pitch), f32),
            pltpu.VMEM((tile_a, pitch), f32),
            pltpu.VMEM((6, tile_a + 2, tile_r, pitch), f32),
            pltpu.VMEM((tile_a, tile_r, pitch), f32),
            pltpu.VMEM((comps, tile_a, tile_r, pitch), f32),
            pltpu.VMEM((nodes, 2 * nodes), bf16),
            pltpu.VMEM((2 * comps * TOP, depth), bf16),
            pltpu.VMEM((tile_a, depth, 2 * pitch), bf16),
            pltpu.VMEM((tile_a, depth, 2 * pitch), bf16),
            pltpu.VMEM((n_tiles, 2 * pitch, TILE), bf16),
            pltpu.VMEM((n_tiles, nodes // 2, TILE), f32),
            pltpu.VMEM((count_k, owned // pitch, pitch), f32),
            pltpu.VMEM((own_tiles, 3, count_k, TILE), f32),
            pltpu.VMEM((3 * nodes, 2 * pitch), bf16),
            pltpu.VMEM((n_tiles, 3, TILE), f32),
            pltpu.VMEM((n_phase, own_tiles, 3, TILE), f32),
            dma((tile_a + 7,)),
            dma((ITERS, 6)),
            dma((ITERS, 6)),
            dma((4,)),
            dma((4,)),
            dma((n_phase,)),
            dma((n_phase,)),
        ],
        compiler_params=pltpu.CompilerParams(
            collective_id=0, has_side_effects=True, vmem_limit_bytes=60 * 1024 * 1024
        ),
    )(
        psi_start[0],
        source[0],
        face_coef,
        diag_coef,
        jnp.transpose(flux_jac, (2, 3, 1, 0)),
        omega,
        metric,
        mode_shape,
        phase_weight,
        pairing[0],
        owner_order[0],
    )
    results = (psi_out, sens)
    psi_out, sens = pl.pallas_call(
        hand_on,
        out_shape=tuple(jax.ShapeDtypeStruct(value.shape, value.dtype) for value in results),
        in_specs=[hbm, hbm],
        out_specs=(hbm, hbm),
        scratch_shapes=[pltpu.VMEM(value.shape, value.dtype) for value in results]
        + [dma((2, 1 + comps // 2))],
        compiler_params=pltpu.CompilerParams(vmem_limit_bytes=60 * 1024 * 1024),
    )(psi_out, sens)
    return (psi_out[None], sens.reshape(count_k, 1, 1, owned))


def solution(mesh):
    sizes = tuple(mesh.shape[name] for name in ("phase", "axial", "radial"))
    assert sizes[1] == 2
    return jax.shard_map(
        functools.partial(body, sizes),
        mesh=mesh,
        in_specs=(
            P("phase", None, "axial", "radial", None),
            P("phase", None, "axial", "radial", None),
            P(None, "axial", "radial", None),
            P("axial", "radial", None),
            P(),
            P(),
            P(),
            P(None, None, "axial", "radial", None),
            P("phase"),
            P("axial", "radial", None),
            P("axial", "radial", None),
        ),
        out_specs=(P("phase", None, "axial", "radial", None), P(None, "axial", "radial", "phase")),
        check_vma=False,
    )
```

```python
import functools
import math

import jax
import jax.numpy as jnp
from jax import lax
from jax.experimental import pallas as pl
from jax.experimental.pallas import tpu as pltpu
from jax.sharding import PartitionSpec as P

BLADES = 16
ITERS = 4
RELAX = 0.8
MESH = pl.DeviceIdType.MESH
TILE = 256
TOP = 8


def split(value):
    high = value.astype(jnp.bfloat16)
    return high, (value - high.astype(jnp.float32)).astype(jnp.bfloat16)


def kernel(
    sizes,
    psi_in,
    source_in,
    face_in,
    diag_in,
    flux_in,
    omega_ref,
    metric_ref,
    mode_in,
    weight_ref,
    pairing_in,
    owner_in,
    out_ref,
    sens_ref,
    psi,
    source_ref,
    face_ref,
    diag_ref,
    flux_ref,
    mode_ref,
    pairing_ref,
    owner_ref,
    radial_sent,
    radial_low,
    radial_high,
    face_sent,
    face_low,
    face_high,
    coef,
    inverse,
    wrapped,
    pair_matrix,
    matrix,
    field_high,
    field_low,
    one_hot,
    row_mask,
    sens,
    modes_owned,
    weighted,
    gathered,
    received,
    load_sem,
    send_sem,
    recv_sem,
    face_send_sem,
    face_recv_sem,
    phase_send_sem,
    phase_recv_sem,
):
    n_phase, n_axial, n_radial = sizes
    comps, tile_a, tile_r, pitch = source_ref.shape
    half = comps // 2
    nodes = tile_a * tile_r
    fold = nodes // 2
    n_tiles = owner_ref.shape[1] // TILE
    own_tiles = n_tiles // n_phase
    n_modes = mode_ref.shape[0]
    depth = 6 * comps * TOP
    phase = lax.axis_index("phase")
    ax = lax.axis_index("axial")
    rad = lax.axis_index("radial")
    has_low = (ax > 0, rad > 0)
    has_high = (ax < n_axial - 1, rad < n_radial - 1)
    rows = pl.ds(TOP, tile_r)

    loads = [
        pltpu.make_async_copy(psi_in.at[:, a], psi.at[0, a + 1, :, rows, :], load_sem.at[a])
        for a in range(tile_a)
    ]
    for pair in (
        (face_in, face_ref),
        (flux_in, flux_ref),
        (pairing_in, pairing_ref),
        (diag_in, diag_ref),
        (owner_in, owner_ref),
        (source_in, source_ref),
        (mode_in, mode_ref),
    ):
        loads.append(pltpu.make_async_copy(pair[0], pair[1], load_sem.at[len(loads)]))
    for copy in loads:
        copy.start()

    barrier = pltpu.get_barrier_semaphore()
    for k in range(1, n_phase):
        pl.semaphore_signal(
            barrier,
            inc=1,
            device_id={"phase": lax.rem(phase + k, n_phase)},
            device_id_type=MESH,
        )
    for name, me, low, high in (
        ("axial", ax, has_low[0], has_high[0]),
        ("radial", rad, has_low[1], has_high[1]),
    ):
        @pl.when(low)
        def _():
            pl.semaphore_signal(barrier, inc=1, device_id={name: me - 1}, device_id_type=MESH)

        @pl.when(high)
        def _():
            pl.semaphore_signal(barrier, inc=1, device_id={name: me + 1}, device_id_type=MESH)

    beyond = tile_a + 1 - jnp.where(ax > 0, 0, tile_a + 1)
    coef[jnp.where(ax > 0, 1, 0), beyond] = jnp.zeros((tile_r, pitch), jnp.float32)
    for s in range(ITERS):
        for c in range(comps):
            psi[s, beyond, c, TOP : TOP + tile_r, :] = jnp.zeros((tile_r, pitch), jnp.float32)

    edge = jnp.where(ax > 0, 1, tile_a)
    halo = jnp.where(ax > 0, 0, tile_a + 1)
    first = jnp.where(ax > 0, 2, 1)

    def layer(k):
        return first + k if k < tile_a - 1 else edge

    def half_rows(k):
        return pl.ds(TOP + k * TOP, TOP)

    def axial_copy(s, k, arriving=False, source=None):
        return pltpu.make_async_remote_copy(
            src_ref=psi.at[s, edge, :, half_rows(k), :] if source is None else source,
            dst_ref=psi.at[s, halo if arriving else tile_a + 1 - halo, :, half_rows(k), :],
            send_sem=send_sem.at[s, k],
            recv_sem=recv_sem.at[s, k],
            device_id={"axial": 1 - ax},
            device_id_type=MESH,
        )

    def radial_copy(s, up, part):
        slots = pl.ds(0, tile_a - 1) if part == 0 else pl.ds(tile_a - 1, 1)
        at = 2 + part * 2 + (0 if up else 1)
        return pltpu.make_async_remote_copy(
            src_ref=radial_sent.at[s, 0 if up else 1, slots],
            dst_ref=(radial_low if up else radial_high).at[s, slots],
            send_sem=send_sem.at[s, at],
            recv_sem=recv_sem.at[s, at],
            device_id={"radial": rad + 1 if up else rad - 1},
            device_id_type=MESH,
        )

    leaving = jnp.where(ax > 0, 1, 0)
    axial_face = 0

    def face_copy(d, arriving=False):
        up = d % 2 == 0
        if d < 2:
            src = coef.at[leaving, edge]
            dst = coef.at[1 - leaving, halo] if arriving else coef.at[leaving, tile_a + 1 - halo]
            target = {"axial": 1 - ax}
        else:
            src = face_sent.at[d - 2]
            dst = face_low if up else face_high
            target = {"radial": rad + 1 if up else rad - 1}
        return pltpu.make_async_remote_copy(
            src_ref=src,
            dst_ref=dst,
            send_sem=face_send_sem.at[d],
            recv_sem=face_recv_sem.at[d],
            device_id=target,
            device_id_type=MESH,
        )

    parts = (range(tile_a - 1), range(tile_a - 1, tile_a))

    def start_radial(s, part):
        for k in parts[part]:
            radial_sent[s, 0, k] = psi[s, layer(k), :, TOP + tile_r - 1, :]
            radial_sent[s, 1, k] = psi[s, layer(k), :, TOP, :]
        for up in (True, False):
            @pl.when((has_high if up else has_low)[1])
            def _():
                radial_copy(s, up, part).start()

    greeted = n_phase - 1 + sum(jnp.where(flag, 1, 0) for flag in has_low + has_high)
    pl.semaphore_wait(barrier, greeted)
    for k in range(2):
        axial_copy(0, k, source=psi_in.at[:, edge - 1, pl.ds(k * TOP, TOP), :]).start()
    for copy in loads[:tile_a]:
        copy.wait()
    for part in range(2):
        start_radial(0, part)

    loads[tile_a].wait()
    for a in range(tile_a):
        for d in range(6):
            coef[d, a + 1] = face_ref[d, a].astype(jnp.float32)
    for a in range(tile_a):
        face_sent[0, a : a + 1, :] = coef[2, a + 1, tile_r - 1 : tile_r, :]
        face_sent[1, a : a + 1, :] = coef[3, a + 1, 0:1, :]
    face_copy(axial_face).start()
    for d in (2, 3):
        @pl.when((has_high if d == 2 else has_low)[1])
        def _():
            face_copy(d).start()

    loads[tile_a + 1].wait()
    real = [flux_ref[j, :, 0, :] for j in range(half)]
    imag = [flux_ref[j, :, 1, :] for j in range(half)]
    fine = lax.Precision.HIGHEST
    entries = (
        jnp.concatenate(real + imag, axis=1),
        jnp.concatenate([-value for value in imag] + real, axis=1),
    )
    tall, wide = comps * TOP, matrix.shape[1]
    spread = jnp.zeros((tall, 6 * comps), jnp.float32)
    row = lax.div(lax.broadcasted_iota(jnp.int32, (tall, half), 0), TOP)
    column = lax.broadcasted_iota(jnp.int32, (tall, half), 1)
    for k in range(2):
        pick = jnp.where(row == column + k * half, 1.0, 0.0)
        spread = spread + jnp.dot(
            pick, entries[k], precision=fine, preferred_element_type=jnp.float32
        )
    row = lax.broadcasted_iota(jnp.int32, (6 * comps, wide), 0)
    column = lax.div(lax.broadcasted_iota(jnp.int32, (6 * comps, wide), 1), TOP)
    spread = jnp.dot(
        spread,
        jnp.where(row == column, 1.0, 0.0),
        precision=fine,
        preferred_element_type=jnp.float32,
    )
    row = lax.rem(lax.broadcasted_iota(jnp.int32, (tall, wide), 0), TOP)
    column = lax.rem(lax.broadcasted_iota(jnp.int32, (tall, wide), 1), TOP)
    high, low = split(jnp.where(row == column, spread, 0.0))
    matrix[:tall] = high
    matrix[tall:] = low
    for slot in range(tile_a):
        for field in (field_high, field_low):
            field[slot, depth:, :] = jnp.zeros((wide - depth, 2 * pitch), jnp.bfloat16)

    loads[tile_a + 2].wait()
    node = lax.broadcasted_iota(jnp.int32, (2 * nodes, nodes), 0)
    partner = jnp.where(node >= nodes, node - nodes, node) == pairing_ref[...]
    pair_matrix[...] = jnp.where(partner, 1.0, 0.0).T.astype(jnp.bfloat16)

    angle = 2.0 * math.pi / BLADES
    turn = lax.rem(phase, BLADES)
    cosine = jnp.float32(1.0)
    sine = jnp.float32(0.0)
    for k in range(1, BLADES):
        cosine = jnp.where(turn == k, jnp.float32(math.cos(angle * k)), cosine)
        sine = jnp.where(turn == k, jnp.float32(math.sin(angle * k)), sine)

    def permuted(value):
        stacked = jnp.concatenate(split(value), axis=0)
        return jnp.dot(pair_matrix[...], stacked, preferred_element_type=jnp.float32)

    lane = lax.broadcasted_iota(jnp.int32, (tile_r, pitch), 1)
    for d, from_lane in ((4, pitch - 1), (5, 0)):
        partner_face = permuted(coef[d, 1 : tile_a + 1].reshape(nodes, pitch))
        for a in range(tile_a):
            own = jnp.where(
                lane == from_lane, partner_face[a * tile_r : (a + 1) * tile_r], coef[d, a + 1]
            )
            coef[d, a + 1] = pltpu.roll(own, 1 if d == 4 else pitch - 1, 1)

    loads[tile_a + 3].wait()
    for a in range(tile_a):
        inverse[a] = RELAX / diag_ref[a]

    shift = pitch.bit_length() - 1

    def make_one_hot(v, _):
        for k in range(2):
            t = lax.rem(phase * own_tiles + 2 * v + k, n_tiles)
            owner = owner_ref[:, pl.ds(pl.multiple_of(t * TILE, TILE), TILE)]
            row = owner >> shift
            column = owner & (pitch - 1)
            column = jnp.where(row >= fold, column + pitch, column)
            row = row & (fold - 1)
            at = lax.broadcasted_iota(jnp.int32, (2 * pitch, TILE), 0)
            at, column = at.astype(jnp.bfloat16), column.astype(jnp.bfloat16)
            one, zero = jnp.bfloat16(1.0), jnp.bfloat16(0.0)
            one_hot[t] = jnp.where(at == column, one, zero)
            at = lax.broadcasted_iota(jnp.int32, (fold, TILE), 0)
            row_mask[t] = jnp.where(at == row, 1.0, 0.0)
        return 0

    def gather_modes(i, _):
        t = phase * own_tiles + i
        for d in range(3):
            for k in range(0, n_modes, 6):
                part = mode_ref[k : k + 6, d].reshape(6, nodes, pitch)
                left = part[:, :fold].reshape(6 * fold, pitch)
                right = part[:, fold:].reshape(6 * fold, pitch)
                picked = jnp.dot(
                    jnp.concatenate([left, right], axis=1),
                    one_hot[t],
                    preferred_element_type=jnp.float32,
                )
                picked = picked.reshape(6, fold, TILE) * row_mask[t][None]
                modes_owned[i, d, k : k + 6, :] = jnp.sum(picked, axis=1)
        return 0

    low_lane = lane[:TOP]

    def build(s, a, slot, halves):
        for k in halves:
            columns = slice(k * pitch, (k + 1) * pitch)
            here = slice(k * TOP, (k + 1) * TOP)

            def field(layer_at, c, shift):
                at = TOP + k * TOP + shift
                return psi[s, layer_at, c, at : at + TOP, :]

            for c in range(comps):
                own = field(a, c, 0)
                wrap = wrapped[c, a - 1, here]
                scaled = (
                    coef[0, a - 1, here] * field(a - 1, c, 0),
                    coef[1, a + 1, here] * field(a + 1, c, 0),
                    coef[2, a, here] * field(a, c, -1),
                    coef[3, a, here] * field(a, c, 1),
                    coef[4, a, here] * pltpu.roll(jnp.where(low_lane == pitch - 1, wrap, own), 1, 1),
                    coef[5, a, here]
                    * pltpu.roll(jnp.where(low_lane == 0, wrap, own), pitch - 1, 1),
                )
                for d in range(0, 6, 2):
                    at = (c * 6 + d) * TOP
                    high, low = split(jnp.concatenate(scaled[d : d + 2], axis=0))
                    field_high[slot, at : at + 2 * TOP, columns] = high
                    field_low[slot, at : at + 2 * TOP, columns] = low

    def update(s, a, slot, halves):
        columns = slice(halves[0] * pitch, (halves[-1] + 1) * pitch)
        both = jnp.dot(
            matrix[...], field_high[slot, :, columns], preferred_element_type=jnp.float32
        )
        rest = jnp.dot(
            matrix[:tall], field_low[slot, :, columns], preferred_element_type=jnp.float32
        )
        total = both[:tall] + (both[tall:] + rest)
        omega = omega_ref[0]
        for n, k in enumerate(halves):
            here = slice(k * TOP, (k + 1) * TOP)
            there = slice(TOP + k * TOP, 2 * TOP + k * TOP)
            scale = inverse[a - 1, here]

            def incoming(c):
                return total[c * TOP : (c + 1) * TOP, n * pitch : (n + 1) * pitch]

            for i in range(half):
                real = psi[s, a, i, there, :]
                imag = psi[s, a, half + i, there, :]
                got_real = source_ref[i, a - 1, here] - omega * imag + incoming(i)
                got_imag = source_ref[half + i, a - 1, here] + omega * real + incoming(half + i)
                psi[s + 1, a, i, there, :] = (1.0 - RELAX) * real + scale * got_real
                psi[s + 1, a, half + i, there, :] = (1.0 - RELAX) * imag + scale * got_imag

    face_lane = lax.broadcasted_iota(jnp.int32, (nodes, pitch), 1)
    turned_sine = jnp.where(face_lane >= pitch // 2, sine, -sine)

    def place_radial(s, part):
        for up in (True, False):
            flag = (has_low if up else has_high)[1]
            at = TOP - 1 if up else TOP + tile_r
            got = radial_low if up else radial_high

            @pl.when(flag)
            def _():
                radial_copy(s, up, part).wait_recv()
                for k in parts[part]:
                    psi[s, layer(k), :, at, :] = got[s, k]

            @pl.when(jnp.logical_not(flag))
            def _():
                for k in parts[part]:
                    psi[s, layer(k), :, at, :] = jnp.zeros((comps, pitch), jnp.float32)

    def section(s, _):
        for j in range(half):
            pair = [
                psi[s, 1 : tile_a + 1, c, TOP : TOP + tile_r, :].reshape(nodes, pitch)
                for c in (j, half + j)
            ]
            both = permuted(jnp.concatenate(pair, axis=1))
            real, imag = both[:, :pitch], both[:, pitch:]
            turned = (cosine * real - turned_sine * imag, turned_sine * real + cosine * imag)
            for c, value in zip((j, half + j), turned):
                wrapped[c] = value.reshape(tile_a, tile_r, pitch)

        @pl.when(s == 0)
        def _():
            for copy in loads[tile_a + 4 :]:
                copy.wait()

        place_radial(s, 0)

        @pl.when(s == 0)
        def _():
            for d in (2, 3):
                flag = (has_low if d == 2 else has_high)[1]
                got = face_low if d == 2 else face_high

                @pl.when(flag)
                def _():
                    face_copy(d).wait_recv()

                row = lax.broadcasted_iota(jnp.int32, (tile_r, pitch), 0)
                end = 0 if d == 2 else tile_r - 1
                for a in range(tile_a):
                    moved = pltpu.roll(coef[d, a + 1], 1 if d == 2 else tile_r - 1, 0)
                    coef[d, a + 1] = jnp.where(row == end, 0.0, moved)

                @pl.when(flag)
                def _():
                    for a in range(tile_a):
                        coef[d, a + 1, end : end + 1, :] = got[a : a + 1, :]

        for k in range(tile_a - 1):
            build(s, layer(k), k, (0, 1))
        for k in range(tile_a - 1):
            update(s, layer(k), k, (0, 1))

        @pl.when(s + 1 < ITERS)
        def _():
            start_radial(s + 1, 0)

        lax.fori_loop(
            lax.div(n_tiles * s, 2 * ITERS), lax.div(n_tiles * (s + 1), 2 * ITERS), make_one_hot, 0
        )
        lax.fori_loop(
            lax.div(own_tiles * s, 2 * ITERS),
            lax.div(own_tiles * (s + 1), 2 * ITERS),
            gather_modes,
            0,
        )
        place_radial(s, 1)

        @pl.when(s == 0)
        def _():
            face_copy(axial_face, arriving=True).wait_recv()

        for k in range(2):
            axial_copy(s, k, arriving=True).wait_recv()
        build(s, edge, tile_a - 1, (0, 1))
        update(s, edge, tile_a - 1, (0, 1))

        @pl.when(s + 1 < ITERS)
        def _():
            for k in range(2):
                axial_copy(s + 1, k).start()

        @pl.when(s + 1 < ITERS)
        def _():
            start_radial(s + 1, 1)

        return 0

    lax.fori_loop(0, ITERS, section, 0)

    results = [
        pltpu.make_async_copy(psi.at[ITERS, a + 1, :, rows, :], out_ref.at[:, a], load_sem.at[a])
        for a in range(tile_a)
    ]
    for copy in results:
        copy.start()

    share = weight_ref[0]
    for a in range(tile_a):
        values = [psi[ITERS, a + 1, c, TOP : TOP + tile_r, :] for c in range(comps)]
        row = (a * tile_r) % fold
        column = pitch * ((a * tile_r) // fold)
        for d in range(3):
            height = metric_ref[d, 0] * values[0]
            for c in range(1, comps):
                height = height + metric_ref[d, c] * values[c]
            for part, value in enumerate(split(share * height)):
                at = (part * 3 + d) * fold + row
                weighted[at : at + tile_r, column : column + pitch] = value

    def gather_weighted(t):
        picked = jnp.dot(weighted[...], one_hot[t], preferred_element_type=jnp.float32)
        picked = picked.reshape(2, 3, fold, TILE)
        gathered[t] = jnp.sum((picked[0] + picked[1]) * row_mask[t][None], axis=1)

    def phase_copy(k):
        peer = lax.rem(phase + k, n_phase)
        return pltpu.make_async_remote_copy(
            src_ref=gathered.at[pl.ds(peer * own_tiles, own_tiles)],
            dst_ref=received.at[k],
            send_sem=phase_send_sem.at[k],
            recv_sem=phase_recv_sem.at[k],
            device_id={"phase": peer},
            device_id_type=MESH,
        )

    for k in list(range(1, n_phase)) + [0]:
        peer = lax.rem(phase + k, n_phase)
        for i in range(own_tiles):
            gather_weighted(peer * own_tiles + i)
        if k:
            phase_copy(k).start()

    lax.fori_loop(own_tiles // 2, own_tiles, gather_modes, 0)

    for k in range(1, n_phase):
        phase_copy(k).wait_recv()

    for i in range(own_tiles):
        total = gathered[phase * own_tiles + i]
        for k in range(1, n_phase):
            total = total + received[k, i]
        result = modes_owned[i, 0] * total[0:1]
        for d in range(1, 3):
            result = result + modes_owned[i, d] * total[d : d + 1]
        for k in range(TILE // pitch):
            sens[:, i * (TILE // pitch) + k, :] = result[:, k * pitch : (k + 1) * pitch]

    results.append(pltpu.make_async_copy(sens, sens_ref, load_sem.at[tile_a]))
    results[-1].start()
    for k in range(1, n_phase):
        phase_copy(k).wait_send()
    face_copy(axial_face).wait_send()
    for s in range(ITERS):
        for k in range(2):
            from_input = psi_in.at[:, edge - 1, pl.ds(k * TOP, TOP), :] if s == 0 else None
            axial_copy(s, k, source=from_input).wait_send()
    for up in (True, False):
        @pl.when((has_high if up else has_low)[1])
        def _():
            face_copy(2 if up else 3).wait_send()
            for s in range(ITERS):
                for part in range(2):
                    radial_copy(s, up, part).wait_send()

    for copy in results:
        copy.wait()


def hand_on(psi_in, sens_in, psi_out, sens_out, psi, sens, sem):
    steps = [(sens_in, sens, sens_out)]
    for c in range(0, psi_in.shape[0], 2):
        own = pl.ds(c, 2)
        steps.append((psi_in.at[own], psi.at[own], psi_out.at[own]))
    arrive = [pltpu.make_async_copy(p, q, sem.at[0, k]) for k, (p, q, _) in enumerate(steps)]
    leave = [pltpu.make_async_copy(q, r, sem.at[1, k]) for k, (_, q, r) in enumerate(steps)]
    for copy in arrive:
        copy.start()
    for k in range(len(steps)):
        arrive[k].wait()
        leave[k].start()
    for copy in leave:
        copy.wait()


def body(
    sizes,
    psi_start,
    source,
    face_coef,
    diag_coef,
    flux_jac,
    omega,
    metric,
    mode_shape,
    phase_weight,
    pairing,
    owner_order,
):
    _, comps, tile_a, tile_r, pitch = psi_start.shape
    half = comps // 2
    nodes = tile_a * tile_r
    cells = nodes * pitch
    n_phase = sizes[0]
    n_tiles = cells // TILE
    own_tiles = n_tiles // n_phase
    owned = cells // n_phase
    count_k = mode_shape.shape[0]
    f32, bf16 = jnp.float32, jnp.bfloat16
    smem = pl.BlockSpec(memory_space=pltpu.SMEM)
    hbm = pl.BlockSpec(memory_space=pltpu.HBM)
    dma = pltpu.SemaphoreType.DMA
    depth = -(-6 * comps * TOP // 128) * 128
    psi_out, sens = pl.pallas_call(
        functools.partial(kernel, sizes),
        out_shape=(
            jax.ShapeDtypeStruct((comps, tile_a, tile_r, pitch), f32),
            jax.ShapeDtypeStruct((count_k, owned // pitch, pitch), f32),
        ),
        in_specs=[hbm, hbm, hbm, hbm, hbm, smem, smem, hbm, smem, hbm, hbm],
        out_specs=(hbm, hbm),
        scratch_shapes=[
            pltpu.VMEM((ITERS + 1, tile_a + 2, comps, tile_r + 2 * TOP, pitch), f32),
            pltpu.VMEM((comps, tile_a, tile_r, pitch), f32),
            pltpu.VMEM((6, tile_a, tile_r, pitch), bf16),
            pltpu.VMEM((tile_a, tile_r, pitch), f32),
            pltpu.VMEM((half, half, 2, 6), f32),
            pltpu.VMEM((count_k, 3, tile_a, tile_r, pitch), bf16),
            pltpu.VMEM((1, nodes), jnp.int32),
            pltpu.VMEM((1, cells), jnp.int32),
            pltpu.VMEM((ITERS, 2, tile_a, comps, pitch), f32),
            pltpu.VMEM((ITERS, tile_a, comps, pitch), f32),
            pltpu.VMEM((ITERS, tile_a, comps, pitch), f32),
            pltpu.VMEM((2, tile_a, pitch), f32),
            pltpu.VMEM((tile_a, pitch), f32),
            pltpu.VMEM((tile_a, pitch), f32),
            pltpu.VMEM((6, tile_a + 2, tile_r, pitch), f32),
            pltpu.VMEM((tile_a, tile_r, pitch), f32),
            pltpu.VMEM((comps, tile_a, tile_r, pitch), f32),
            pltpu.VMEM((nodes, 2 * nodes), bf16),
            pltpu.VMEM((2 * comps * TOP, depth), bf16),
            pltpu.VMEM((tile_a, depth, 2 * pitch), bf16),
            pltpu.VMEM((tile_a, depth, 2 * pitch), bf16),
            pltpu.VMEM((n_tiles, 2 * pitch, TILE), bf16),
            pltpu.VMEM((n_tiles, nodes // 2, TILE), f32),
            pltpu.VMEM((count_k, owned // pitch, pitch), f32),
            pltpu.VMEM((own_tiles, 3, count_k, TILE), f32),
            pltpu.VMEM((3 * nodes, 2 * pitch), bf16),
            pltpu.VMEM((n_tiles, 3, TILE), f32),
            pltpu.VMEM((n_phase, own_tiles, 3, TILE), f32),
            dma((tile_a + 7,)),
            dma((ITERS, 6)),
            dma((ITERS, 6)),
            dma((4,)),
            dma((4,)),
            dma((n_phase,)),
            dma((n_phase,)),
        ],
        compiler_params=pltpu.CompilerParams(
            collective_id=0, has_side_effects=True, vmem_limit_bytes=60 * 1024 * 1024
        ),
    )(
        psi_start[0],
        source[0],
        face_coef,
        diag_coef,
        jnp.transpose(flux_jac, (2, 3, 1, 0)),
        omega,
        metric,
        mode_shape,
        phase_weight,
        pairing[0],
        owner_order[0],
    )
    results = (psi_out, sens)
    psi_out, sens = pl.pallas_call(
        hand_on,
        out_shape=tuple(jax.ShapeDtypeStruct(value.shape, value.dtype) for value in results),
        in_specs=[hbm, hbm],
        out_specs=(hbm, hbm),
        scratch_shapes=[pltpu.VMEM(value.shape, value.dtype) for value in results]
        + [dma((2, 1 + comps // 2))],
        compiler_params=pltpu.CompilerParams(vmem_limit_bytes=60 * 1024 * 1024),
    )(psi_out, sens)
    return (psi_out[None], sens.reshape(count_k, 1, 1, owned))


def solution(mesh):
    sizes = tuple(mesh.shape[name] for name in ("phase", "axial", "radial"))
    assert sizes[1] == 2
    return jax.shard_map(
        functools.partial(body, sizes),
        mesh=mesh,
        in_specs=(
            P("phase", None, "axial", "radial", None),
            P("phase", None, "axial", "radial", None),
            P(None, "axial", "radial", None),
            P("axial", "radial", None),
            P(),
            P(),
            P(),
            P(None, None, "axial", "radial", None),
            P("phase"),
            P("axial", "radial", None),
            P("axial", "radial", None),
        ),
        out_specs=(P("phase", None, "axial", "radial", None), P(None, "axial", "radial", "phase")),
        check_vma=False,
    )
```
